32 devices in a mesh: lon: 8 (over y, x, core), lat: 4 (over z).
Axes of the slice: x: 2, y: 2, z: 4, core: 2. Of those that a mesh axis runs over, the one named last changes fastest.
Arguments:
- velocity: float32 [2, 4, 256, 4096], P(None, None, 'lat', 'lon'), may hold values from -3 to 3
- thickness: float32 [4, 256, 4096], P(None, 'lat', 'lon'), may hold values from -6 to 6
- tracers: float32 [2, 4, 256, 4096], P(None, None, 'lat', 'lon'), may hold values from -6 to 6
- land_mask: int32 [4, 256, 4096], P(None, 'lat', 'lon'), may hold values from 0 to 1, as said below
Outputs:
- velocity_out: float32 [2, 4, 256, 4096], P(None, None, 'lat', 'lon')
- thickness_out: float32 [4, 256, 4096], P(None, 'lat', 'lon')
- tracers_out: float32 [2, 4, 256, 4096], P(None, None, 'lat', 'lon')
The draws below stay inside these ranges and needn't reach their ends.
Inputs may be any that keep to these rules, and one draw needn't show every extreme that they name: `land_mask`: A level is ocean only where every level above it is ocean.
All inputs are finite; a program needn't handle non-finite values.
Results may differ from the reference program's by a relative error of at most 0.00002.
Values sent between devices are 32-bit elements; how exact they have to be, the bound alone decides.
No kernel may reach another device: no remote copies, remote signals or barrier semaphores. Data moves between devices by JAX's collectives and lax.ppermute only.
A program may use at most 64 MiB of HBM per device.

```python
import jax
import jax.numpy as jnp
from jax import lax

K = 4
STEPS = 2
NX = 4096
NY = 256


def draw_land_mask(key, part):
    depth_level = jax.random.randint(key, (NY, NX), 0, K + 3)
    levels = jnp.arange(K, dtype=jnp.int32)[:, None, None]
    return (depth_level[None] > levels).astype(jnp.int32)


def level_of(rng, dims, cuts, low, largest):
    level, own = 1.0, jax.random.fold_in(rng, 6)
    for position, shards_of in cuts:
        steps = jnp.exp(jax.random.uniform(jax.random.fold_in(own, position), (shards_of,), jnp.float32, low / len(cuts), largest / len(cuts)))
        level = level * jnp.repeat(steps, dims[position] // shards_of).reshape([-1 if axis == position else 1 for axis in range(len(dims))])
    return level


def gaussian(own_key, extent, deviation, bound, split=(), held_as=jnp.bfloat16):
    values = deviation * jax.random.normal(own_key, extent, jnp.float32)
    if split:
        values = values * level_of(own_key, extent, split, -0.22, 0.18)
    return jnp.clip(values, -bound, bound).astype(held_as)


def setup_inputs(seed: int = 0) -> dict:
    keys = jax.random.split(jax.random.key(seed), 5)
    return {
        "velocity": gaussian(keys[0], (2, K, NY, NX), 0.5, 3.0, ((2, 4), (3, 8)), jnp.float32),
        "thickness": gaussian(keys[1], (K, NY, NX), 1.0, 6.0, ((1, 4), (2, 8)), jnp.float32),
        "tracers": gaussian(keys[2], (2, K, NY, NX), 1.0, 6.0, ((2, 4), (3, 8)), jnp.float32),
        "land_mask": draw_land_mask(jax.random.fold_in(keys[4], 71), 0),
    }


ADVECTION = 0.25
DIFFUSION = 0.05
HYPERVISCOSITY = 0.02
CORIOLIS = 0.3
GRADIENT = 0.2
CONVERGENCE = 0.3


def laplace(values):
    return (values[..., 2:, 1:-1] + values[..., :-2, 1:-1] + values[..., 1:-1, 2:]
            + values[..., 1:-1, :-2] - 4.0 * values[..., 1:-1, 1:-1])


def diff_east(values):
    return 0.5 * (values[..., 1:-1, 2:] - values[..., 1:-1, :-2])


def diff_north(values):
    return 0.5 * (values[..., 2:, 1:-1] - values[..., :-2, 1:-1])


def pressure(planes):
    levels = planes.shape[1]
    weights = (1.0 / (jnp.arange(levels, dtype=jnp.float32) + 1.0))[:, None, None]
    return jnp.cumsum(weights * planes[2] + 0.1 * (0.8 * planes[4] - planes[3]), axis=0)


def coriolis_rows(row_ids, total_rows):
    folded = jnp.where(row_ids >= total_rows, 2 * total_rows - 1 - row_ids, row_ids)
    angle = jnp.pi * (folded.astype(jnp.float32) + 0.5) / total_rows - jnp.pi / 2
    return jnp.sin(angle)[:, None]


def step_core(planes, pressure_field, mask_cut, coriolis):
    padded_one = planes[..., 1:-1, 1:-1]
    centre = planes[..., 2:-2, 2:-2]
    lap_one = laplace(planes)
    biharmonic = laplace(lap_one)
    lap_centre = lap_one[..., 1:-1, 1:-1]
    east_vel = centre[0]
    north_vel = centre[1]
    advection = east_vel * diff_east(padded_one) + north_vel * diff_north(padded_one)
    updated = centre - ADVECTION * advection + DIFFUSION * lap_centre - HYPERVISCOSITY * biharmonic
    press_one = pressure_field[..., 1:-1, 1:-1]
    divergence = diff_east(padded_one[0]) + diff_north(padded_one[1])
    new_east = updated[0] + CORIOLIS * coriolis * north_vel - GRADIENT * diff_east(press_one)
    new_north = updated[1] - CORIOLIS * coriolis * east_vel - GRADIENT * diff_north(press_one)
    new_thick = updated[2] - CONVERGENCE * divergence
    return jnp.stack([new_east, new_north, new_thick, updated[3], updated[4]]) * mask_cut


def extend_global(fields, flip_signs, halo_width):
    widened = jnp.concatenate([fields[..., -halo_width:], fields, fields[..., :halo_width]], -1)
    north_rows = flip_signs * widened[..., ::-1, ::-1][..., :halo_width, :]
    south_rows = jnp.zeros_like(north_rows)
    return jnp.concatenate([south_rows, widened, north_rows], -2)


def reference(velocity, thickness, tracers, land_mask):
    fields = jnp.concatenate([velocity, thickness[None], tracers], 0)
    mask_float = land_mask.astype(jnp.float32)
    total_rows = fields.shape[2]
    coriolis = coriolis_rows(jnp.arange(total_rows, dtype=jnp.int32), total_rows)
    flip_signs = jnp.array([-1.0, -1.0, 1.0, 1.0, 1.0], dtype=jnp.float32)[:, None, None, None]
    for step_num in range(STEPS):
        padded = extend_global(fields, flip_signs, 2)
        pressure_field = pressure(padded)

        def one_level(level_num):
            return step_core(padded[:, level_num], pressure_field[level_num], mask_float[level_num], coriolis)

        stacked = lax.map(one_level, jnp.arange(K, dtype=jnp.int32))
        fields = jnp.swapaxes(stacked, 0, 1)
    return fields[0:2], fields[2], fields[3:5]
```

```python
import functools

import jax
import jax.numpy as jnp
from jax import lax
from jax.experimental import pallas as pl
from jax.experimental.pallas import tpu as pltpu
from jax.sharding import PartitionSpec as P

ADVECTION = 0.25
DIFFUSION = 0.05
HYPERVISCOSITY = 0.02
CORIOLIS = 0.3
GRADIENT = 0.2
CONVERGENCE = 0.3

HALO = 4
PAD = 8
LANES = 128
SUB = 8
SLOTS = 11
F32 = jnp.float32
VMEM = pl.BlockSpec(memory_space=pltpu.VMEM)
HBM = pl.BlockSpec(memory_space=pltpu.HBM)
ANY = pl.BlockSpec(memory_space=pl.ANY)


def even_half(lanes):
    return lax.broadcasted_iota(jnp.int32, (SUB, lanes), 0) % 2 == 0


def flip_lanes(values):
    index = LANES - 1 - lax.broadcasted_iota(jnp.int32, (SUB, LANES), 1)
    chunks = range(0, values.shape[-1], LANES)
    parts = [jnp.take_along_axis(values[:, c : c + LANES], index, axis=1) for c in reversed(chunks)]
    return jnp.concatenate(parts, axis=1)


def run_copies(copies):
    for copy in copies:
        copy.start()
    for copy in copies:
        copy.wait()


def columns_kernel(vel, thick, trac, mask, out_a, out_b, edges, land, sem):
    levels, rows, width = thick.shape
    half_rows = rows // 2
    copies = []
    for side in range(2):
        lanes = pl.ds(side * (width - LANES), LANES)
        to = pl.ds(side * LANES, LANES)
        for level in range(levels):
            for half in range(2):
                at, s = pl.ds(half * half_rows, half_rows), 2 * level + half
                for source, target in (
                    (vel.at[:, level, at, lanes], edges.at[0:2, :, s, to]),
                    (thick.at[level, at, lanes], edges.at[2, :, s, to]),
                    (trac.at[:, level, at, lanes], edges.at[3:5, :, s, to]),
                    (mask.at[level, at, lanes], land.at[:, s, to]),
                ):
                    copies.append(pltpu.make_async_copy(source, target, sem))
    run_copies(copies)
    lon_even = lax.axis_index("lon") % 2 == 0
    group = lax.broadcasted_iota(jnp.int32, (SUB, LANES), 1) // HALO
    for f in range(6):
        west = east = jnp.zeros((SUB, LANES), F32)
        for row in range(half_rows):
            pair = edges[f, row] if f < 5 else land[row].astype(F32)
            here = group == row
            west = jnp.where(here, pltpu.roll(pair[:, :LANES], HALO * row % LANES, 1), west)
            east = jnp.where(here, pltpu.roll(pair[:, LANES:], HALO * (row + 1) % LANES, 1), east)
        out_a[f] = jnp.where(lon_even, east, west)
        out_b[f] = jnp.where(lon_even, west, east)


def load_kernel(lat_count, vel, thick, trac, mask, after, planes, coriolis, land, sem):
    del after
    levels, rows, width = thick.shape
    half_rows = rows // 2
    length = half_rows + PAD
    copies = []
    for level in range(levels):
        for half in range(2):
            at, s = pl.ds(half * (half_rows - PAD), length), 2 * level + half
            to = pl.ds((1 - half) * PAD, length)
            for source, target in (
                (vel.at[:, level, at, :], planes.at[0:2, to, s, :]),
                (thick.at[level, at, :], planes.at[2, to, s, :]),
                (trac.at[:, level, at, :], planes.at[3:5, to, s, :]),
                (mask.at[level, at, :], land.at[to, s, :]),
            ):
                copies.append(pltpu.make_async_copy(source, target, sem))
    for copy in copies:
        copy.start()
    total = rows * lat_count
    half = lax.broadcasted_iota(jnp.int32, (SUB, LANES), 0) % 2
    first = lax.axis_index("lat") * rows + half * half_rows
    for row in range(-2, half_rows + 2):
        ids = first + row
        folded = jnp.where(ids >= total, 2 * total - 1 - ids, ids)
        angle = jnp.pi * (folded.astype(F32) + 0.5) / total - jnp.pi / 2
        coriolis[row + PAD] = jnp.sin(angle)
    for copy in copies:
        copy.wait()
    for row in range(PAD - 2, half_rows + PAD + 2):
        planes[5, row] = land[row].astype(F32)


def halo_columns(cols_a, cols_b, lon_even):
    lane = lax.broadcasted_iota(jnp.int32, (SUB, LANES), 1)

    def get(f):
        a, b = cols_a[f], cols_b[f]
        from_west = jnp.where(lon_even, b, a)
        from_east = jnp.where(lon_even, a, b)

        def row(r):
            east = pltpu.roll(from_east, -HALO * r % LANES, 1)
            west = pltpu.roll(from_west, -HALO * (r + 1) % LANES, 1)
            return jnp.where(lane < LANES // 2, east, west)

        return row

    return get


def rows_kernel(lat_count, planes, cols_a, cols_b, out_a, out_b):
    half_rows, width = planes.shape[1] - 2 * PAD, planes.shape[3]
    chunks = width // LANES
    lat = lax.axis_index("lat")
    lat_even = lat % 2 == 0
    lon_even = lax.axis_index("lon") % 2 == 0
    even = even_half(width + LANES)
    group = lax.broadcasted_iota(jnp.int32, (SUB, LANES), 1) // 8
    get = halo_columns(cols_a, cols_b, lon_even)
    column = [get(f) for f in range(6)]
    slots = [(f, m) for f in range(5) for m in range(2)] + [(5, None)]

    def whole(f, row):
        return jnp.concatenate([planes[f, row + PAD], column[f](row)], axis=1)

    def north(f, m):
        low = half_rows - HALO + 2 * m
        return jnp.where(even, pltpu.roll(whole(f, low + 1), SUB - 1, 0), whole(f, low))

    def south(f, m):
        return jnp.where(even, whole(f, 2 * m), pltpu.roll(whole(f, 2 * m + 1), 1, 0))

    def put(target, slot, value):
        for c in range(chunks):
            target[chunks * slot + c] = value[:, c * LANES : (c + 1) * LANES]

    def add_corner(corner, slot, value):
        return jnp.where(group == slot, pltpu.roll(value[:, width:], 8 * slot + HALO, 1), corner)

    corner_a = corner_b = jnp.zeros((SUB, LANES), F32)
    for slot, (f, m) in enumerate(slots):
        to_north = north(f, 1 if m is None else m)
        to_south = south(f, 0 if m is None else m)
        a = jnp.where(lat_even, to_north, to_south)
        b = jnp.where(lat_even, to_south, to_north)
        put(out_a, slot, a)
        put(out_b, slot, b)
        corner_a = add_corner(corner_a, slot, a)
        corner_b = add_corner(corner_b, slot, b)
    out_a[chunks * SLOTS] = corner_a
    out_b[chunks * SLOTS] = corner_b

    @pl.when(lat == lat_count - 1)
    def _():
        target = out_a if (lat_count - 1) % 2 == 0 else out_b
        corner = jnp.zeros((SUB, LANES), F32)
        for slot, (f, m) in enumerate(slots):
            value = north(f, 1 if m is None else 1 - m)
            value = -value if f < 2 else value
            mirrored = jnp.concatenate([flip_lanes(value[:, :width]), flip_lanes(value[:, width:])], axis=1)
            put(target, slot, mirrored)
            corner = add_corner(corner, slot, mirrored)
        target[chunks * SLOTS] = corner


def make_step(wide, lap, east_diff, press):
    level = lax.broadcasted_iota(jnp.int32, (SUB, wide), 0) // 2
    weight = 1.0 / (level.astype(F32) + 1.0)
    below_one, below_two = level >= 1, level >= 2

    def shifts(value):
        return pltpu.roll(value, wide - 1, 1), pltpu.roll(value, 1, 1)

    def ahead(source, row):
        at = row + PAD
        centres = [source(f, row) for f in range(5)]
        for f in range(5):
            to_east, to_west = shifts(centres[f])
            lap[f, at] = (
                (to_east + to_west) + (source(f, row + 1) + source(f, row - 1)) - 4.0 * centres[f]
            )
            east_diff[f, at] = to_east - to_west
        part = weight * centres[2] + 0.1 * (0.8 * centres[4] - centres[3])
        part = part + jnp.where(below_one, pltpu.roll(part, 2, 0), 0.0)
        press[at] = part + jnp.where(below_two, pltpu.roll(part, 4, 0), 0.0)

    def update(source, ocean, coriolis, row, cut, emit):
        at = row + PAD
        lanes = slice(0, cut)
        u, v = source(0, row)[:, lanes], source(1, row)[:, lanes]
        half_u, half_v = (-0.5 * ADVECTION) * u, (-0.5 * ADVECTION) * v
        p_east, p_west = shifts(press[at])
        slope_east = (-0.5 * GRADIENT) * (p_east - p_west)[:, lanes]
        slope_north = (-0.5 * GRADIENT) * (press[at + 1, :, lanes] - press[at - 1, :, lanes])
        turn = jnp.concatenate([CORIOLIS * coriolis] * (cut // LANES), axis=1)
        for f in range(5):
            dx = east_diff[f, at, :, lanes]
            dy = source(f, row + 1)[:, lanes] - source(f, row - 1)[:, lanes]
            if f == 0:
                u_east = dx
            if f == 1:
                v_north = dy
            here = lap[f, at]
            l_east, l_west = shifts(here)
            around = (l_east + l_west)[:, lanes] + (
                lap[f, at + 1, :, lanes] + lap[f, at - 1, :, lanes]
            )
            value = source(f, row)[:, lanes] + (half_u * dx + half_v * dy)
            value = value + (
                (DIFFUSION + 4.0 * HYPERVISCOSITY) * here[:, lanes] - HYPERVISCOSITY * around
            )
            if f == 0:
                value = value + (turn * v + slope_east)
            if f == 1:
                value = value + (slope_north - turn * u)
            if f == 2:
                value = value - (0.5 * CONVERGENCE) * (u_east + v_north)
            emit(f, row, value * ocean)

    return ahead, update


def interior_kernel(planes, cols_a, cols_b, coriolis, after, out, ring, outer, second, lap, east_diff, press):
    del after
    half_rows, width = planes.shape[1] - 2 * PAD, planes.shape[3]
    wide = width + LANES
    lon_even = lax.axis_index("lon") % 2 == 0
    get = halo_columns(cols_a, cols_b, lon_even)
    for f in range(6):
        column = get(f)
        for row in range(half_rows):
            value = column(row)
            outer[f, row + PAD] = value
            if row < HALO:
                outer[f, row + PAD + half_rows] = pltpu.roll(value, SUB - 1, 0)
            if row >= half_rows - HALO:
                outer[f, row + PAD - half_rows] = pltpu.roll(value, 1, 0)
    ahead, update = make_step(wide, lap, east_diff, press)

    def whole(f, row):
        return jnp.concatenate([planes[f, row + PAD], outer[f, row + PAD]], axis=1)

    def keep(f, row, value):
        second[f, row + PAD] = value

    def halfway(f, row):
        return second[f, row + PAD]

    def write(f, row, value):
        out[f, row] = value

    def sweep(source, low, high, cut, emit):
        ahead(source, low - 1)
        ahead(source, low)

        def iteration(row, carry):
            ahead(source, row + 1)
            ocean = whole(5, row)[:, :cut]
            update(source, ocean, coriolis[row + PAD], row, cut, emit)
            return carry

        lax.fori_loop(low, high, iteration, 0)

    sweep(whole, 2, half_rows - 2, wide, keep)
    for f in range(5):
        for i in range(4):
            ring[f, i] = second[f, 2 + i + PAD]
            ring[f, 4 + i] = second[f, half_rows - 6 + i + PAD]
    sweep(halfway, HALO, half_rows - HALO, width, write)


def edges_kernel(
    planes, outer, coriolis, done, ring, rows_a, rows_b, vel_out, thick_out, trac_out, strip, second, lap, east_diff, press, sem
):
    half_rows, width = planes.shape[1] - 2 * PAD, planes.shape[3]
    wide = width + LANES
    chunks = width // LANES
    levels = SUB // 2

    def copies_out(source, source_row, row, count):
        copies = []
        for level in range(levels):
            for half in range(2):
                s = 2 * level + half
                rows, to = pl.ds(source_row, count), pl.ds(half * half_rows + row, count)
                copies += [
                    pltpu.make_async_copy(source.at[0:2, rows, s, :], vel_out.at[:, level, to, :], sem),
                    pltpu.make_async_copy(source.at[2, rows, s, :], thick_out.at[level, to, :], sem),
                    pltpu.make_async_copy(source.at[3:5, rows, s, :], trac_out.at[:, level, to, :], sem),
                ]
        for copy in copies:
            copy.start()
        return copies

    copies = copies_out(done, PAD, PAD, half_rows - 2 * PAD)
    for f in range(5):
        for i in range(HALO):
            strip[f, HALO + i] = done[f, HALO + i]
            strip[f, PAD + i] = done[f, half_rows - PAD + i]
    lat_even = lax.axis_index("lat") % 2 == 0
    even = even_half(wide)
    corner_a, corner_b = rows_a[chunks * SLOTS], rows_b[chunks * SLOTS]

    def message(ref, corner, slot):
        parts = [ref[chunks * slot + c] for c in range(chunks)]
        return jnp.concatenate([*parts, pltpu.roll(corner, -(8 * slot + HALO) % LANES, 1)], axis=1)

    south, north = {}, {}
    for f in range(6):
        reach = HALO if f < 5 else 2
        for m in range(reach // 2):
            slot = 2 * f + m
            a, b = message(rows_a, corner_a, slot), message(rows_b, corner_b, slot)
            from_south = jnp.where(lat_even, b, a)
            from_north = jnp.where(lat_even, a, b)
            south[f, 2 * m - reach] = pltpu.roll(from_south, SUB - 1, 0)
            south[f, 2 * m - reach + 1] = from_south
            north[f, half_rows + 2 * m] = pltpu.roll(from_north, 1, 0)
            north[f, half_rows + 2 * m + 1] = from_north

    def whole(f, row):
        own = jnp.concatenate([planes[f, row + PAD], outer[f, row + PAD]], axis=1)
        if row < 0:
            return jnp.where(even, south[f, row], own)
        if row >= half_rows:
            return jnp.where(even, own, north[f, row])
        return own

    ahead, update = make_step(wide, lap, east_diff, press)

    def halfway(f, row):
        if 2 <= row < 6:
            return ring[f, row - 2]
        if half_rows - 6 <= row < half_rows - 2:
            return ring[f, row - (half_rows - 6) + 4]
        return second[f, row + PAD]

    def keep(f, row, value):
        second[f, row + PAD] = value

    def write(f, row, value):
        strip[f, row if row < HALO else row - half_rows + 2 * PAD] = value

    def sweep(source, low, high, cut, emit):
        ahead(source, low - 1)
        ahead(source, low)
        for row in range(low, high):
            ahead(source, row + 1)
            update(source, whole(5, row)[:, :cut], coriolis[row + PAD], row, cut, emit)

    sweep(whole, -2, 2, wide, keep)
    sweep(halfway, 0, HALO, width, write)
    copies += copies_out(strip, 0, 0, PAD)
    sweep(whole, half_rows - 2, half_rows + 2, wide, keep)
    sweep(halfway, half_rows - HALO, half_rows, width, write)
    copies += copies_out(strip, PAD, half_rows - PAD, PAD)
    for copy in copies:
        copy.wait()


def lat_pairs(parity, lat_count, lon_count):
    pairs = []
    for lat in range(lat_count):
        for lon in range(lon_count):
            to_lat, to_lon = (lat + 1 if lat % 2 == parity else lat - 1), lon
            if to_lat < 0:
                continue
            if to_lat == lat_count:
                to_lat, to_lon = lat, lon_count - 1 - lon
            pairs.append((lon * lat_count + lat, to_lon * lat_count + to_lat))
    return pairs


def lon_pairs(parity, lon_count):
    return [(i, (i + 1 if i % 2 == parity else i - 1) % lon_count) for i in range(lon_count)]


def shapes(*dims):
    return jax.ShapeDtypeStruct(dims, F32)


def body(lat_count, lon_count, velocity, thickness, tracers, land_mask):
    levels, rows, width = thickness.shape
    half_rows = rows // 2
    wide, tall = width + LANES, half_rows + 2 * PAD
    fields = (velocity, thickness, tracers, land_mask)
    dma = pltpu.SemaphoreType.DMA

    def call(kernel, name, in_specs, outs, out_specs, scratch, flops):
        return pl.pallas_call(
            kernel,
            out_shape=outs,
            in_specs=in_specs,
            out_specs=out_specs,
            scratch_shapes=scratch,
            compiler_params=pltpu.CompilerParams(vmem_limit_bytes=40 * 2**20),
            cost_estimate=pl.CostEstimate(flops=flops, bytes_accessed=flops // 10, transcendentals=0),
            name=name,
        )

    columns = shapes(6, SUB, LANES)
    send_a, send_b = call(
        columns_kernel,
        "pack_columns",
        [HBM] * 4,
        (columns, columns),
        (VMEM, VMEM),
        [pltpu.VMEM((5, half_rows, SUB, 2 * LANES), F32), pltpu.VMEM((half_rows, SUB, 2 * LANES), jnp.int32), dma],
        10**6,
    )(*fields)
    cols_a = lax.ppermute(send_a, "lon", lon_pairs(0, lon_count))
    cols_b = lax.ppermute(send_b, "lon", lon_pairs(1, lon_count))

    planes, coriolis = call(
        functools.partial(load_kernel, lat_count),
        "load_fields",
        [HBM, HBM, HBM, HBM, ANY],
        (shapes(6, tall, SUB, width), shapes(tall, SUB, LANES)),
        (VMEM, VMEM),
        [pltpu.VMEM((tall, SUB, width), jnp.int32), dma],
        10**8,
    )(*fields, send_a)

    message = shapes(SLOTS * (width // LANES) + 1, SUB, LANES)
    send_a, send_b = call(
        functools.partial(rows_kernel, lat_count),
        "pack_rows",
        [VMEM] * 3,
        (message, message),
        (VMEM, VMEM),
        [],
        10**6,
    )(planes, cols_a, cols_b)
    axes = ("lon", "lat")
    rows_a = lax.ppermute(send_a, axes, lat_pairs(0, lat_count, lon_count))
    rows_b = lax.ppermute(send_b, axes, lat_pairs(1, lat_count, lon_count))

    wide_planes = pltpu.VMEM((5, tall, SUB, wide), F32)
    work = [wide_planes, wide_planes, wide_planes, pltpu.VMEM((tall, SUB, wide), F32)]
    done, ring, outer = call(
        interior_kernel,
        "interior",
        [VMEM, VMEM, VMEM, VMEM, ANY],
        (shapes(5, half_rows, SUB, width), shapes(5, 8, SUB, wide), shapes(6, tall, SUB, LANES)),
        (VMEM, VMEM, VMEM),
        work,
        10**8,
    )(planes, cols_a, cols_b, coriolis, send_a)

    return call(
        edges_kernel,
        "edges",
        [VMEM] * 7,
        (shapes(*velocity.shape), shapes(*thickness.shape), shapes(*tracers.shape)),
        (HBM, HBM, HBM),
        [pltpu.VMEM((5, 2 * PAD, SUB, width), F32), *work, dma],
        10**8,
    )(planes, outer, coriolis, done, ring, rows_a, rows_b)


def solution(mesh):
    specs = (P(None, None, "lat", "lon"), P(None, "lat", "lon"), P(None, None, "lat", "lon"))
    return jax.shard_map(
        functools.partial(body, mesh.shape["lat"], mesh.shape["lon"]),
        mesh=mesh,
        in_specs=(*specs, P(None, "lat", "lon")),
        out_specs=specs,
        check_vma=False,
    )
```

```python
import functools

import jax
import jax.numpy as jnp
from jax import lax
from jax.experimental import pallas as pl
from jax.experimental.pallas import tpu as pltpu
from jax.sharding import PartitionSpec as P

ADVECTION = 0.25
DIFFUSION = 0.05
HYPERVISCOSITY = 0.02
CORIOLIS = 0.3
GRADIENT = 0.2
CONVERGENCE = 0.3

HALO = 4
PAD = 8
LANES = 128
SUB = 8
SLOTS = 11
F32 = jnp.float32
VMEM = pl.BlockSpec(memory_space=pltpu.VMEM)
HBM = pl.BlockSpec(memory_space=pltpu.HBM)
ANY = pl.BlockSpec(memory_space=pl.ANY)


def even_half(lanes):
    return lax.broadcasted_iota(jnp.int32, (SUB, lanes), 0) % 2 == 0


def flip_lanes(values):
    index = LANES - 1 - lax.broadcasted_iota(jnp.int32, (SUB, LANES), 1)
    chunks = range(0, values.shape[-1], LANES)
    parts = [jnp.take_along_axis(values[:, c : c + LANES], index, axis=1) for c in reversed(chunks)]
    return jnp.concatenate(parts, axis=1)


def run_copies(copies):
    for copy in copies:
        copy.start()
    for copy in copies:
        copy.wait()


def columns_kernel(vel, thick, trac, mask, out_a, out_b, edges, land, sem):
    levels, rows, width = thick.shape
    half_rows = rows // 2
    copies = []
    for side in range(2):
        lanes = pl.ds(side * (width - LANES), LANES)
        to = pl.ds(side * LANES, LANES)
        for level in range(levels):
            for half in range(2):
                at, s = pl.ds(half * half_rows, half_rows), 2 * level + half
                for source, target in (
                    (vel.at[:, level, at, lanes], edges.at[0:2, :, s, to]),
                    (thick.at[level, at, lanes], edges.at[2, :, s, to]),
                    (trac.at[:, level, at, lanes], edges.at[3:5, :, s, to]),
                    (mask.at[level, at, lanes], land.at[:, s, to]),
                ):
                    copies.append(pltpu.make_async_copy(source, target, sem))
    run_copies(copies)
    lon_even = lax.axis_index("lon") % 2 == 0
    group = lax.broadcasted_iota(jnp.int32, (SUB, LANES), 1) // HALO
    for f in range(6):
        west = east = jnp.zeros((SUB, LANES), F32)
        for row in range(half_rows):
            pair = edges[f, row] if f < 5 else land[row].astype(F32)
            here = group == row
            west = jnp.where(here, pltpu.roll(pair[:, :LANES], HALO * row % LANES, 1), west)
            east = jnp.where(here, pltpu.roll(pair[:, LANES:], HALO * (row + 1) % LANES, 1), east)
        out_a[f] = jnp.where(lon_even, east, west)
        out_b[f] = jnp.where(lon_even, west, east)


def load_kernel(lat_count, vel, thick, trac, mask, after, planes, coriolis, land, sem):
    del after
    levels, rows, width = thick.shape
    half_rows = rows // 2
    length = half_rows + PAD
    copies = []
    for level in range(levels):
        for half in range(2):
            at, s = pl.ds(half * (half_rows - PAD), length), 2 * level + half
            to = pl.ds((1 - half) * PAD, length)
            for source, target in (
                (vel.at[:, level, at, :], planes.at[0:2, to, s, :]),
                (thick.at[level, at, :], planes.at[2, to, s, :]),
                (trac.at[:, level, at, :], planes.at[3:5, to, s, :]),
                (mask.at[level, at, :], land.at[to, s, :]),
            ):
                copies.append(pltpu.make_async_copy(source, target, sem))
    for copy in copies:
        copy.start()
    total = rows * lat_count
    half = lax.broadcasted_iota(jnp.int32, (SUB, LANES), 0) % 2
    first = lax.axis_index("lat") * rows + half * half_rows
    for row in range(-2, half_rows + 2):
        ids = first + row
        folded = jnp.where(ids >= total, 2 * total - 1 - ids, ids)
        angle = jnp.pi * (folded.astype(F32) + 0.5) / total - jnp.pi / 2
        coriolis[row + PAD] = jnp.sin(angle)
    for copy in copies:
        copy.wait()
    for row in range(PAD - 2, half_rows + PAD + 2):
        planes[5, row] = land[row].astype(F32)


def halo_columns(cols_a, cols_b, lon_even):
    lane = lax.broadcasted_iota(jnp.int32, (SUB, LANES), 1)

    def get(f):
        a, b = cols_a[f], cols_b[f]
        from_west = jnp.where(lon_even, b, a)
        from_east = jnp.where(lon_even, a, b)

        def row(r):
            east = pltpu.roll(from_east, -HALO * r % LANES, 1)
            west = pltpu.roll(from_west, -HALO * (r + 1) % LANES, 1)
            return jnp.where(lane < LANES // 2, east, west)

        return row

    return get


def rows_kernel(lat_count, planes, cols_a, cols_b, out_a, out_b):
    half_rows, width = planes.shape[1] - 2 * PAD, planes.shape[3]
    chunks = width // LANES
    lat = lax.axis_index("lat")
    lat_even = lat % 2 == 0
    lon_even = lax.axis_index("lon") % 2 == 0
    even = even_half(width + LANES)
    group = lax.broadcasted_iota(jnp.int32, (SUB, LANES), 1) // 8
    get = halo_columns(cols_a, cols_b, lon_even)
    column = [get(f) for f in range(6)]
    slots = [(f, m) for f in range(5) for m in range(2)] + [(5, None)]

    def whole(f, row):
        return jnp.concatenate([planes[f, row + PAD], column[f](row)], axis=1)

    def north(f, m):
        low = half_rows - HALO + 2 * m
        return jnp.where(even, pltpu.roll(whole(f, low + 1), SUB - 1, 0), whole(f, low))

    def south(f, m):
        return jnp.where(even, whole(f, 2 * m), pltpu.roll(whole(f, 2 * m + 1), 1, 0))

    def put(target, slot, value):
        for c in range(chunks):
            target[chunks * slot + c] = value[:, c * LANES : (c + 1) * LANES]

    def add_corner(corner, slot, value):
        return jnp.where(group == slot, pltpu.roll(value[:, width:], 8 * slot + HALO, 1), corner)

    corner_a = corner_b = jnp.zeros((SUB, LANES), F32)
    for slot, (f, m) in enumerate(slots):
        to_north = north(f, 1 if m is None else m)
        to_south = south(f, 0 if m is None else m)
        a = jnp.where(lat_even, to_north, to_south)
        b = jnp.where(lat_even, to_south, to_north)
        put(out_a, slot, a)
        put(out_b, slot, b)
        corner_a = add_corner(corner_a, slot, a)
        corner_b = add_corner(corner_b, slot, b)
    out_a[chunks * SLOTS] = corner_a
    out_b[chunks * SLOTS] = corner_b

    @pl.when(lat == lat_count - 1)
    def _():
        target = out_a if (lat_count - 1) % 2 == 0 else out_b
        corner = jnp.zeros((SUB, LANES), F32)
        for slot, (f, m) in enumerate(slots):
            value = north(f, 1 if m is None else 1 - m)
            value = -value if f < 2 else value
            mirrored = jnp.concatenate([flip_lanes(value[:, :width]), flip_lanes(value[:, width:])], axis=1)
            put(target, slot, mirrored)
            corner = add_corner(corner, slot, mirrored)
        target[chunks * SLOTS] = corner


def make_step(wide, lap, east_diff, press):
    level = lax.broadcasted_iota(jnp.int32, (SUB, wide), 0) // 2
    weight = 1.0 / (level.astype(F32) + 1.0)
    below_one, below_two = level >= 1, level >= 2

    def shifts(value):
        return pltpu.roll(value, wide - 1, 1), pltpu.roll(value, 1, 1)

    def ahead(source, row):
        at = row + PAD
        centres = [source(f, row) for f in range(5)]
        for f in range(5):
            to_east, to_west = shifts(centres[f])
            lap[f, at] = (
                (to_east + to_west) + (source(f, row + 1) + source(f, row - 1)) - 4.0 * centres[f]
            )
            east_diff[f, at] = to_east - to_west
        part = weight * centres[2] + 0.1 * (0.8 * centres[4] - centres[3])
        part = part + jnp.where(below_one, pltpu.roll(part, 2, 0), 0.0)
        press[at] = part + jnp.where(below_two, pltpu.roll(part, 4, 0), 0.0)

    def update(source, ocean, coriolis, row, cut, emit):
        at = row + PAD
        lanes = slice(0, cut)
        u, v = source(0, row)[:, lanes], source(1, row)[:, lanes]
        half_u, half_v = (-0.5 * ADVECTION) * u, (-0.5 * ADVECTION) * v
        p_east, p_west = shifts(press[at])
        slope_east = (-0.5 * GRADIENT) * (p_east - p_west)[:, lanes]
        slope_north = (-0.5 * GRADIENT) * (press[at + 1, :, lanes] - press[at - 1, :, lanes])
        turn = jnp.concatenate([CORIOLIS * coriolis] * (cut // LANES), axis=1)
        for f in range(5):
            dx = east_diff[f, at, :, lanes]
            dy = source(f, row + 1)[:, lanes] - source(f, row - 1)[:, lanes]
            if f == 0:
                u_east = dx
            if f == 1:
                v_north = dy
            here = lap[f, at]
            l_east, l_west = shifts(here)
            around = (l_east + l_west)[:, lanes] + (
                lap[f, at + 1, :, lanes] + lap[f, at - 1, :, lanes]
            )
            value = source(f, row)[:, lanes] + (half_u * dx + half_v * dy)
            value = value + (
                (DIFFUSION + 4.0 * HYPERVISCOSITY) * here[:, lanes] - HYPERVISCOSITY * around
            )
            if f == 0:
                value = value + (turn * v + slope_east)
            if f == 1:
                value = value + (slope_north - turn * u)
            if f == 2:
                value = value - (0.5 * CONVERGENCE) * (u_east + v_north)
            emit(f, row, value * ocean)

    return ahead, update


def interior_kernel(planes, cols_a, cols_b, coriolis, after, out, ring, outer, second, lap, east_diff, press):
    del after
    half_rows, width = planes.shape[1] - 2 * PAD, planes.shape[3]
    wide = width + LANES
    lon_even = lax.axis_index("lon") % 2 == 0
    get = halo_columns(cols_a, cols_b, lon_even)
    for f in range(6):
        column = get(f)
        for row in range(half_rows):
            value = column(row)
            outer[f, row + PAD] = value
            if row < HALO:
                outer[f, row + PAD + half_rows] = pltpu.roll(value, SUB - 1, 0)
            if row >= half_rows - HALO:
                outer[f, row + PAD - half_rows] = pltpu.roll(value, 1, 0)
    ahead, update = make_step(wide, lap, east_diff, press)

    def whole(f, row):
        return jnp.concatenate([planes[f, row + PAD], outer[f, row + PAD]], axis=1)

    def keep(f, row, value):
        second[f, row + PAD] = value

    def halfway(f, row):
        return second[f, row + PAD]

    def write(f, row, value):
        out[f, row] = value

    def sweep(source, low, high, cut, emit):
        ahead(source, low - 1)
        ahead(source, low)

        def iteration(row, carry):
            ahead(source, row + 1)
            ocean = whole(5, row)[:, :cut]
            update(source, ocean, coriolis[row + PAD], row, cut, emit)
            return carry

        lax.fori_loop(low, high, iteration, 0)

    sweep(whole, 2, half_rows - 2, wide, keep)
    for f in range(5):
        for i in range(4):
            ring[f, i] = second[f, 2 + i + PAD]
            ring[f, 4 + i] = second[f, half_rows - 6 + i + PAD]
    sweep(halfway, HALO, half_rows - HALO, width, write)


def edges_kernel(
    planes, outer, coriolis, done, ring, rows_a, rows_b, vel_out, thick_out, trac_out, strip, second, lap, east_diff, press, sem
):
    half_rows, width = planes.shape[1] - 2 * PAD, planes.shape[3]
    wide = width + LANES
    chunks = width // LANES
    levels = SUB // 2

    def copies_out(source, source_row, row, count):
        copies = []
        for level in range(levels):
            for half in range(2):
                s = 2 * level + half
                rows, to = pl.ds(source_row, count), pl.ds(half * half_rows + row, count)
                copies += [
                    pltpu.make_async_copy(source.at[0:2, rows, s, :], vel_out.at[:, level, to, :], sem),
                    pltpu.make_async_copy(source.at[2, rows, s, :], thick_out.at[level, to, :], sem),
                    pltpu.make_async_copy(source.at[3:5, rows, s, :], trac_out.at[:, level, to, :], sem),
                ]
        for copy in copies:
            copy.start()
        return copies

    copies = copies_out(done, PAD, PAD, half_rows - 2 * PAD)
    for f in range(5):
        for i in range(HALO):
            strip[f, HALO + i] = done[f, HALO + i]
            strip[f, PAD + i] = done[f, half_rows - PAD + i]
    lat_even = lax.axis_index("lat") % 2 == 0
    even = even_half(wide)
    corner_a, corner_b = rows_a[chunks * SLOTS], rows_b[chunks * SLOTS]

    def message(ref, corner, slot):
        parts = [ref[chunks * slot + c] for c in range(chunks)]
        return jnp.concatenate([*parts, pltpu.roll(corner, -(8 * slot + HALO) % LANES, 1)], axis=1)

    south, north = {}, {}
    for f in range(6):
        reach = HALO if f < 5 else 2
        for m in range(reach // 2):
            slot = 2 * f + m
            a, b = message(rows_a, corner_a, slot), message(rows_b, corner_b, slot)
            from_south = jnp.where(lat_even, b, a)
            from_north = jnp.where(lat_even, a, b)
            south[f, 2 * m - reach] = pltpu.roll(from_south, SUB - 1, 0)
            south[f, 2 * m - reach + 1] = from_south
            north[f, half_rows + 2 * m] = pltpu.roll(from_north, 1, 0)
            north[f, half_rows + 2 * m + 1] = from_north

    def whole(f, row):
        own = jnp.concatenate([planes[f, row + PAD], outer[f, row + PAD]], axis=1)
        if row < 0:
            return jnp.where(even, south[f, row], own)
        if row >= half_rows:
            return jnp.where(even, own, north[f, row])
        return own

    ahead, update = make_step(wide, lap, east_diff, press)

    def halfway(f, row):
        if 2 <= row < 6:
            return ring[f, row - 2]
        if half_rows - 6 <= row < half_rows - 2:
            return ring[f, row - (half_rows - 6) + 4]
        return second[f, row + PAD]

    def keep(f, row, value):
        second[f, row + PAD] = value

    def write(f, row, value):
        strip[f, row if row < HALO else row - half_rows + 2 * PAD] = value

    def sweep(source, low, high, cut, emit):
        ahead(source, low - 1)
        ahead(source, low)
        for row in range(low, high):
            ahead(source, row + 1)
            update(source, whole(5, row)[:, :cut], coriolis[row + PAD], row, cut, emit)

    sweep(whole, -2, 2, wide, keep)
    sweep(halfway, 0, HALO, width, write)
    copies += copies_out(strip, 0, 0, PAD)
    sweep(whole, half_rows - 2, half_rows + 2, wide, keep)
    sweep(halfway, half_rows - HALO, half_rows, width, write)
    copies += copies_out(strip, PAD, half_rows - PAD, PAD)
    for copy in copies:
        copy.wait()


def lat_pairs(parity, lat_count, lon_count):
    pairs = []
    for lat in range(lat_count):
        for lon in range(lon_count):
            to_lat, to_lon = (lat + 1 if lat % 2 == parity else lat - 1), lon
            if to_lat < 0:
                continue
            if to_lat == lat_count:
                to_lat, to_lon = lat, lon_count - 1 - lon
            pairs.append((lon * lat_count + lat, to_lon * lat_count + to_lat))
    return pairs


def lon_pairs(parity, lon_count):
    return [(i, (i + 1 if i % 2 == parity else i - 1) % lon_count) for i in range(lon_count)]


def shapes(*dims):
    return jax.ShapeDtypeStruct(dims, F32)


def body(lat_count, lon_count, velocity, thickness, tracers, land_mask):
    levels, rows, width = thickness.shape
    half_rows = rows // 2
    wide, tall = width + LANES, half_rows + 2 * PAD
    arguments = (velocity, thickness, tracers, land_mask)
    fields = [pltpu.with_memory_space_constraint(x, pltpu.HBM) for x in arguments]
    dma = pltpu.SemaphoreType.DMA

    def call(kernel, name, in_specs, outs, out_specs, scratch, flops):
        return pl.pallas_call(
            kernel,
            out_shape=outs,
            in_specs=in_specs,
            out_specs=out_specs,
            scratch_shapes=scratch,
            compiler_params=pltpu.CompilerParams(vmem_limit_bytes=40 * 2**20),
            cost_estimate=pl.CostEstimate(flops=flops, bytes_accessed=flops // 10, transcendentals=0),
            name=name,
        )

    columns = shapes(6, SUB, LANES)
    send_a, send_b = call(
        columns_kernel,
        "pack_columns",
        [HBM] * 4,
        (columns, columns),
        (VMEM, VMEM),
        [pltpu.VMEM((5, half_rows, SUB, 2 * LANES), F32), pltpu.VMEM((half_rows, SUB, 2 * LANES), jnp.int32), dma],
        10**6,
    )(*fields)
    cols_a = lax.ppermute(send_a, "lon", lon_pairs(0, lon_count))
    cols_b = lax.ppermute(send_b, "lon", lon_pairs(1, lon_count))

    planes, coriolis = call(
        functools.partial(load_kernel, lat_count),
        "load_fields",
        [HBM, HBM, HBM, HBM, ANY],
        (shapes(6, tall, SUB, width), shapes(tall, SUB, LANES)),
        (VMEM, VMEM),
        [pltpu.VMEM((tall, SUB, width), jnp.int32), dma],
        10**8,
    )(*fields, send_a)

    message = shapes(SLOTS * (width // LANES) + 1, SUB, LANES)
    send_a, send_b = call(
        functools.partial(rows_kernel, lat_count),
        "pack_rows",
        [VMEM] * 3,
        (message, message),
        (VMEM, VMEM),
        [],
        10**6,
    )(planes, cols_a, cols_b)
    axes = ("lon", "lat")
    rows_a = lax.ppermute(send_a, axes, lat_pairs(0, lat_count, lon_count))
    rows_b = lax.ppermute(send_b, axes, lat_pairs(1, lat_count, lon_count))

    wide_planes = pltpu.VMEM((5, tall, SUB, wide), F32)
    work = [wide_planes, wide_planes, wide_planes, pltpu.VMEM((tall, SUB, wide), F32)]
    done, ring, outer = call(
        interior_kernel,
        "interior",
        [VMEM, VMEM, VMEM, VMEM, ANY],
        (shapes(5, half_rows, SUB, width), shapes(5, 8, SUB, wide), shapes(6, tall, SUB, LANES)),
        (VMEM, VMEM, VMEM),
        work,
        10**8,
    )(planes, cols_a, cols_b, coriolis, send_a)

    return call(
        edges_kernel,
        "edges",
        [VMEM] * 7,
        (shapes(*velocity.shape), shapes(*thickness.shape), shapes(*tracers.shape)),
        (HBM, HBM, HBM),
        [pltpu.VMEM((5, 2 * PAD, SUB, width), F32), *work, dma],
        10**8,
    )(planes, outer, coriolis, done, ring, rows_a, rows_b)


def solution(mesh):
    specs = (P(None, None, "lat", "lon"), P(None, "lat", "lon"), P(None, None, "lat", "lon"))
    return jax.shard_map(
        functools.partial(body, mesh.shape["lat"], mesh.shape["lon"]),
        mesh=mesh,
        in_specs=(*specs, P(None, "lat", "lon")),
        out_specs=specs,
        check_vma=False,
    )
```

```python
import functools

import jax
import jax.numpy as jnp
from jax import lax
from jax.experimental import pallas as pl
from jax.experimental.pallas import tpu as pltpu
from jax.sharding import PartitionSpec as P

ADVECTION = 0.25
DIFFUSION = 0.05
HYPERVISCOSITY = 0.02
CORIOLIS = 0.3
GRADIENT = 0.2
CONVERGENCE = 0.3

HALO = 4
PAD = 8
LANES = 128
SUB = 8
SLOTS = 11
F32 = jnp.float32
VMEM = pl.BlockSpec(memory_space=pltpu.VMEM)
HBM = pl.BlockSpec(memory_space=pltpu.HBM)
ANY = pl.BlockSpec(memory_space=pl.ANY)


def even_half(lanes):
    return lax.broadcasted_iota(jnp.int32, (SUB, lanes), 0) % 2 == 0


def flip_lanes(values):
    index = LANES - 1 - lax.broadcasted_iota(jnp.int32, (SUB, LANES), 1)
    chunks = range(0, values.shape[-1], LANES)
    parts = [jnp.take_along_axis(values[:, c : c + LANES], index, axis=1) for c in reversed(chunks)]
    return jnp.concatenate(parts, axis=1)


def run_copies(copies):
    for copy in copies:
        copy.start()
    for copy in copies:
        copy.wait()


def columns_kernel(vel, thick, trac, mask, out_a, out_b, edges, land, sem):
    levels, rows, width = thick.shape
    half_rows = rows // 2
    copies = []
    for side in range(2):
        lanes = pl.ds(side * (width - LANES), LANES)
        to = pl.ds(side * LANES, LANES)
        for level in range(levels):
            for half in range(2):
                at, s = pl.ds(half * half_rows, half_rows), 2 * level + half
                for source, target in (
                    (vel.at[:, level, at, lanes], edges.at[0:2, :, s, to]),
                    (thick.at[level, at, lanes], edges.at[2, :, s, to]),
                    (trac.at[:, level, at, lanes], edges.at[3:5, :, s, to]),
                    (mask.at[level, at, lanes], land.at[:, s, to]),
                ):
                    copies.append(pltpu.make_async_copy(source, target, sem))
    run_copies(copies)
    lon_even = lax.axis_index("lon") % 2 == 0
    group = lax.broadcasted_iota(jnp.int32, (SUB, LANES), 1) // HALO
    for f in range(6):
        west = east = jnp.zeros((SUB, LANES), F32)
        for row in range(half_rows):
            pair = edges[f, row] if f < 5 else land[row].astype(F32)
            here = group == row
            west = jnp.where(here, pltpu.roll(pair[:, :LANES], HALO * row % LANES, 1), west)
            east = jnp.where(here, pltpu.roll(pair[:, LANES:], HALO * (row + 1) % LANES, 1), east)
        out_a[f] = jnp.where(lon_even, east, west)
        out_b[f] = jnp.where(lon_even, west, east)


def load_kernel(lat_count, vel, thick, trac, mask, after, planes, coriolis, land, sem):
    del after
    levels, rows, width = thick.shape
    half_rows = rows // 2
    length = half_rows + PAD
    copies = []
    for level in range(levels):
        for half in range(2):
            at, s = pl.ds(half * (half_rows - PAD), length), 2 * level + half
            to = pl.ds((1 - half) * PAD, length)
            for source, target in (
                (vel.at[:, level, at, :], planes.at[0:2, to, s, :]),
                (thick.at[level, at, :], planes.at[2, to, s, :]),
                (trac.at[:, level, at, :], planes.at[3:5, to, s, :]),
                (mask.at[level, at, :], land.at[to, s, :]),
            ):
                copies.append(pltpu.make_async_copy(source, target, sem))
    for copy in copies:
        copy.start()
    total = rows * lat_count
    half = lax.broadcasted_iota(jnp.int32, (SUB, LANES), 0) % 2
    first = lax.axis_index("lat") * rows + half * half_rows
    for row in range(-2, half_rows + 2):
        ids = first + row
        folded = jnp.where(ids >= total, 2 * total - 1 - ids, ids)
        angle = jnp.pi * (folded.astype(F32) + 0.5) / total - jnp.pi / 2
        coriolis[row + PAD] = jnp.sin(angle)
    for copy in copies:
        copy.wait()
    for row in range(PAD - 2, half_rows + PAD + 2):
        planes[5, row] = land[row].astype(F32)


def halo_columns(cols_a, cols_b, lon_even):
    lane = lax.broadcasted_iota(jnp.int32, (SUB, LANES), 1)

    def get(f):
        a, b = cols_a[f], cols_b[f]
        from_west = jnp.where(lon_even, b, a)
        from_east = jnp.where(lon_even, a, b)

        def row(r):
            east = pltpu.roll(from_east, -HALO * r % LANES, 1)
            west = pltpu.roll(from_west, -HALO * (r + 1) % LANES, 1)
            return jnp.where(lane < LANES // 2, east, west)

        return row

    return get


def rows_kernel(lat_count, planes, cols_a, cols_b, out_a, out_b):
    half_rows, width = planes.shape[1] - 2 * PAD, planes.shape[3]
    chunks = width // LANES
    lat = lax.axis_index("lat")
    lat_even = lat % 2 == 0
    lon_even = lax.axis_index("lon") % 2 == 0
    even = even_half(width + LANES)
    group = lax.broadcasted_iota(jnp.int32, (SUB, LANES), 1) // 8
    get = halo_columns(cols_a, cols_b, lon_even)
    column = [get(f) for f in range(6)]
    slots = [(f, m) for f in range(5) for m in range(2)] + [(5, None)]

    def whole(f, row):
        return jnp.concatenate([planes[f, row + PAD], column[f](row)], axis=1)

    def north(f, m):
        low = half_rows - HALO + 2 * m
        return jnp.where(even, pltpu.roll(whole(f, low + 1), SUB - 1, 0), whole(f, low))

    def south(f, m):
        return jnp.where(even, whole(f, 2 * m), pltpu.roll(whole(f, 2 * m + 1), 1, 0))

    def put(target, slot, value):
        for c in range(chunks):
            target[chunks * slot + c] = value[:, c * LANES : (c + 1) * LANES]

    def add_corner(corner, slot, value):
        return jnp.where(group == slot, pltpu.roll(value[:, width:], 8 * slot + HALO, 1), corner)

    corner_a = corner_b = jnp.zeros((SUB, LANES), F32)
    for slot, (f, m) in enumerate(slots):
        to_north = north(f, 1 if m is None else m)
        to_south = south(f, 0 if m is None else m)
        a = jnp.where(lat_even, to_north, to_south)
        b = jnp.where(lat_even, to_south, to_north)
        put(out_a, slot, a)
        put(out_b, slot, b)
        corner_a = add_corner(corner_a, slot, a)
        corner_b = add_corner(corner_b, slot, b)
    out_a[chunks * SLOTS] = corner_a
    out_b[chunks * SLOTS] = corner_b

    @pl.when(lat == lat_count - 1)
    def _():
        target = out_a if (lat_count - 1) % 2 == 0 else out_b
        corner = jnp.zeros((SUB, LANES), F32)
        for slot, (f, m) in enumerate(slots):
            value = north(f, 1 if m is None else 1 - m)
            value = -value if f < 2 else value
            mirrored = jnp.concatenate([flip_lanes(value[:, :width]), flip_lanes(value[:, width:])], axis=1)
            put(target, slot, mirrored)
            corner = add_corner(corner, slot, mirrored)
        target[chunks * SLOTS] = corner


def make_step(wide, lap, east_diff, press):
    level = lax.broadcasted_iota(jnp.int32, (SUB, wide), 0) // 2
    weight = 1.0 / (level.astype(F32) + 1.0)
    below_one, below_two = level >= 1, level >= 2

    def shifts(value):
        return pltpu.roll(value, wide - 1, 1), pltpu.roll(value, 1, 1)

    def ahead(source, row):
        at = row + PAD
        centres = [source(f, row) for f in range(5)]
        for f in range(5):
            to_east, to_west = shifts(centres[f])
            lap[f, at] = (
                (to_east + to_west) + (source(f, row + 1) + source(f, row - 1)) - 4.0 * centres[f]
            )
            east_diff[f, at] = to_east - to_west
        part = weight * centres[2] + 0.1 * (0.8 * centres[4] - centres[3])
        part = part + jnp.where(below_one, pltpu.roll(part, 2, 0), 0.0)
        press[at] = part + jnp.where(below_two, pltpu.roll(part, 4, 0), 0.0)

    def update(source, ocean, coriolis, row, cut, emit):
        at = row + PAD
        lanes = slice(0, cut)
        u, v = source(0, row)[:, lanes], source(1, row)[:, lanes]
        half_u, half_v = (-0.5 * ADVECTION) * u, (-0.5 * ADVECTION) * v
        p_east, p_west = shifts(press[at])
        slope_east = (-0.5 * GRADIENT) * (p_east - p_west)[:, lanes]
        slope_north = (-0.5 * GRADIENT) * (press[at + 1, :, lanes] - press[at - 1, :, lanes])
        turn = jnp.concatenate([CORIOLIS * coriolis] * (cut // LANES), axis=1)
        for f in range(5):
            dx = east_diff[f, at, :, lanes]
            dy = source(f, row + 1)[:, lanes] - source(f, row - 1)[:, lanes]
            if f == 0:
                u_east = dx
            if f == 1:
                v_north = dy
            here = lap[f, at]
            l_east, l_west = shifts(here)
            around = (l_east + l_west)[:, lanes] + (
                lap[f, at + 1, :, lanes] + lap[f, at - 1, :, lanes]
            )
            value = source(f, row)[:, lanes] + (half_u * dx + half_v * dy)
            value = value + (
                (DIFFUSION + 4.0 * HYPERVISCOSITY) * here[:, lanes] - HYPERVISCOSITY * around
            )
            if f == 0:
                value = value + (turn * v + slope_east)
            if f == 1:
                value = value + (slope_north - turn * u)
            if f == 2:
                value = value - (0.5 * CONVERGENCE) * (u_east + v_north)
            emit(f, row, value * ocean)

    return ahead, update


def interior_kernel(planes, cols_a, cols_b, coriolis, after, out, ring, outer, second, lap, east_diff, press):
    del after
    half_rows, width = planes.shape[1] - 2 * PAD, planes.shape[3]
    wide = width + LANES
    lon_even = lax.axis_index("lon") % 2 == 0
    get = halo_columns(cols_a, cols_b, lon_even)
    for f in range(6):
        column = get(f)
        for row in range(half_rows):
            value = column(row)
            outer[f, row + PAD] = value
            if row < HALO:
                outer[f, row + PAD + half_rows] = pltpu.roll(value, SUB - 1, 0)
            if row >= half_rows - HALO:
                outer[f, row + PAD - half_rows] = pltpu.roll(value, 1, 0)
    ahead, update = make_step(wide, lap, east_diff, press)

    def whole(f, row):
        return jnp.concatenate([planes[f, row + PAD], outer[f, row + PAD]], axis=1)

    def keep(f, row, value):
        second[f, row + PAD] = value

    def halfway(f, row):
        return second[f, row + PAD]

    def write(f, row, value):
        out[f, row] = value

    def sweep(source, low, high, cut, emit):
        ahead(source, low - 1)
        ahead(source, low)

        def iteration(row, carry):
            ahead(source, row + 1)
            ocean = whole(5, row)[:, :cut]
            update(source, ocean, coriolis[row + PAD], row, cut, emit)
            return carry

        lax.fori_loop(low, high, iteration, 0, unroll=4)

    sweep(whole, 2, half_rows - 2, wide, keep)
    for f in range(5):
        for i in range(4):
            ring[f, i] = second[f, 2 + i + PAD]
            ring[f, 4 + i] = second[f, half_rows - 6 + i + PAD]
    sweep(halfway, HALO, half_rows - HALO, width, write)


def edges_kernel(
    planes, outer, coriolis, done, ring, rows_a, rows_b, vel_out, thick_out, trac_out, strip, second, lap, east_diff, press, sem
):
    half_rows, width = planes.shape[1] - 2 * PAD, planes.shape[3]
    wide = width + LANES
    chunks = width // LANES
    levels = SUB // 2

    def copies_out(source, source_row, row, count):
        copies = []
        for level in range(levels):
            for half in range(2):
                s = 2 * level + half
                rows, to = pl.ds(source_row, count), pl.ds(half * half_rows + row, count)
                copies += [
                    pltpu.make_async_copy(source.at[0:2, rows, s, :], vel_out.at[:, level, to, :], sem),
                    pltpu.make_async_copy(source.at[2, rows, s, :], thick_out.at[level, to, :], sem),
                    pltpu.make_async_copy(source.at[3:5, rows, s, :], trac_out.at[:, level, to, :], sem),
                ]
        for copy in copies:
            copy.start()
        return copies

    copies = copies_out(done, PAD, PAD, half_rows - 2 * PAD)
    for f in range(5):
        for i in range(HALO):
            strip[f, HALO + i] = done[f, HALO + i]
            strip[f, PAD + i] = done[f, half_rows - PAD + i]
    lat = lax.axis_index("lat")
    lat_even, southmost = lat % 2 == 0, lat == 0
    even = even_half(wide)
    corner_a, corner_b = rows_a[chunks * SLOTS], rows_b[chunks * SLOTS]

    def message(ref, corner, slot):
        parts = [ref[chunks * slot + c] for c in range(chunks)]
        return jnp.concatenate([*parts, pltpu.roll(corner, -(8 * slot + HALO) % LANES, 1)], axis=1)

    south, north = {}, {}
    for f in range(6):
        reach = HALO if f < 5 else 2
        for m in range(reach // 2):
            slot = 2 * f + m
            a, b = message(rows_a, corner_a, slot), message(rows_b, corner_b, slot)
            from_south = jnp.where(southmost, 0.0, jnp.where(lat_even, b, a))
            from_north = jnp.where(lat_even, a, b)
            south[f, 2 * m - reach] = pltpu.roll(from_south, SUB - 1, 0)
            south[f, 2 * m - reach + 1] = from_south
            north[f, half_rows + 2 * m] = pltpu.roll(from_north, 1, 0)
            north[f, half_rows + 2 * m + 1] = from_north

    def whole(f, row):
        own = jnp.concatenate([planes[f, row + PAD], outer[f, row + PAD]], axis=1)
        if row < 0:
            return jnp.where(even, south[f, row], own)
        if row >= half_rows:
            return jnp.where(even, own, north[f, row])
        return own

    ahead, update = make_step(wide, lap, east_diff, press)

    def halfway(f, row):
        if 2 <= row < 6:
            return ring[f, row - 2]
        if half_rows - 6 <= row < half_rows - 2:
            return ring[f, row - (half_rows - 6) + 4]
        return second[f, row + PAD]

    def keep(f, row, value):
        second[f, row + PAD] = value

    def write(f, row, value):
        strip[f, row if row < HALO else row - half_rows + 2 * PAD] = value

    def sweep(source, low, high, cut, emit):
        ahead(source, low - 1)
        ahead(source, low)
        for row in range(low, high):
            ahead(source, row + 1)
            update(source, whole(5, row)[:, :cut], coriolis[row + PAD], row, cut, emit)

    sweep(whole, -2, 2, wide, keep)
    sweep(halfway, 0, HALO, width, write)
    copies += copies_out(strip, 0, 0, PAD)
    sweep(whole, half_rows - 2, half_rows + 2, wide, keep)
    sweep(halfway, half_rows - HALO, half_rows, width, write)
    copies += copies_out(strip, PAD, half_rows - PAD, PAD)
    for copy in copies:
        copy.wait()


def lat_pairs(parity, lat_count, lon_count):
    pairs = []
    for lat in range(lat_count):
        for lon in range(lon_count):
            to_lat, to_lon = (lat + 1 if lat % 2 == parity else lat - 1), lon
            if to_lat < 0:
                to_lat, to_lon = 0, lon ^ 1
            if to_lat == lat_count:
                to_lat, to_lon = lat, lon_count - 1 - lon
            pairs.append((lon * lat_count + lat, to_lon * lat_count + to_lat))
    return pairs


def lon_pairs(parity, lon_count):
    return [(i, (i + 1 if i % 2 == parity else i - 1) % lon_count) for i in range(lon_count)]


def shapes(*dims):
    return jax.ShapeDtypeStruct(dims, F32)


def body(lat_count, lon_count, velocity, thickness, tracers, land_mask):
    levels, rows, width = thickness.shape
    half_rows = rows // 2
    wide, tall = width + LANES, half_rows + 2 * PAD
    arguments = (velocity, thickness, tracers, land_mask)
    fields = [pltpu.with_memory_space_constraint(x, pltpu.HBM) for x in arguments]
    dma = pltpu.SemaphoreType.DMA

    def call(kernel, name, in_specs, outs, out_specs, scratch, flops):
        return pl.pallas_call(
            kernel,
            out_shape=outs,
            in_specs=in_specs,
            out_specs=out_specs,
            scratch_shapes=scratch,
            compiler_params=pltpu.CompilerParams(vmem_limit_bytes=40 * 2**20),
            cost_estimate=pl.CostEstimate(flops=flops, bytes_accessed=flops // 10, transcendentals=0),
            name=name,
        )

    columns = shapes(6, SUB, LANES)
    send_a, send_b = call(
        columns_kernel,
        "pack_columns",
        [HBM] * 4,
        (columns, columns),
        (VMEM, VMEM),
        [pltpu.VMEM((5, half_rows, SUB, 2 * LANES), F32), pltpu.VMEM((half_rows, SUB, 2 * LANES), jnp.int32), dma],
        10**6,
    )(*fields)
    cols_a = lax.ppermute(send_a, "lon", lon_pairs(0, lon_count))
    cols_b = lax.ppermute(send_b, "lon", lon_pairs(1, lon_count))

    planes, coriolis = call(
        functools.partial(load_kernel, lat_count),
        "load_fields",
        [HBM, HBM, HBM, HBM, ANY],
        (shapes(6, tall, SUB, width), shapes(tall, SUB, LANES)),
        (VMEM, VMEM),
        [pltpu.VMEM((tall, SUB, width), jnp.int32), dma],
        10**8,
    )(*fields, send_a)

    message = shapes(SLOTS * (width // LANES) + 1, SUB, LANES)
    send_a, send_b = call(
        functools.partial(rows_kernel, lat_count),
        "pack_rows",
        [VMEM] * 3,
        (message, message),
        (VMEM, VMEM),
        [],
        10**6,
    )(planes, cols_a, cols_b)
    axes = ("lon", "lat")
    rows_a = lax.ppermute(send_a, axes, lat_pairs(0, lat_count, lon_count))
    rows_b = lax.ppermute(send_b, axes, lat_pairs(1, lat_count, lon_count))

    wide_planes = pltpu.VMEM((5, tall, SUB, wide), F32)
    work = [wide_planes, wide_planes, wide_planes, pltpu.VMEM((tall, SUB, wide), F32)]
    done, ring, outer = call(
        interior_kernel,
        "interior",
        [VMEM, VMEM, VMEM, VMEM, ANY],
        (shapes(5, half_rows, SUB, width), shapes(5, 8, SUB, wide), shapes(6, tall, SUB, LANES)),
        (VMEM, VMEM, VMEM),
        work,
        10**8,
    )(planes, cols_a, cols_b, coriolis, send_a)

    return call(
        edges_kernel,
        "edges",
        [VMEM] * 7,
        (shapes(*velocity.shape), shapes(*thickness.shape), shapes(*tracers.shape)),
        (HBM, HBM, HBM),
        [pltpu.VMEM((5, 2 * PAD, SUB, width), F32), *work, dma],
        10**8,
    )(planes, outer, coriolis, done, ring, rows_a, rows_b)


def solution(mesh):
    specs = (P(None, None, "lat", "lon"), P(None, "lat", "lon"), P(None, None, "lat", "lon"))
    return jax.shard_map(
        functools.partial(body, mesh.shape["lat"], mesh.shape["lon"]),
        mesh=mesh,
        in_specs=(*specs, P(None, "lat", "lon")),
        out_specs=specs,
        check_vma=False,
    )
```

```python
import functools

import jax
import jax.numpy as jnp
from jax import lax
from jax.experimental import pallas as pl
from jax.experimental.pallas import tpu as pltpu
from jax.sharding import PartitionSpec as P

ADVECTION = 0.25
DIFFUSION = 0.05
HYPERVISCOSITY = 0.02
CORIOLIS = 0.3
GRADIENT = 0.2
CONVERGENCE = 0.3

HALO = 4
PAD = 8
LANES = 128
SUB = 8
SLOTS = 11
F32 = jnp.float32
VMEM = pl.BlockSpec(memory_space=pltpu.VMEM)
HBM = pl.BlockSpec(memory_space=pltpu.HBM)
ANY = pl.BlockSpec(memory_space=pl.ANY)


def even_half(lanes):
    return lax.broadcasted_iota(jnp.int32, (SUB, lanes), 0) % 2 == 0


def flip_lanes(values):
    index = LANES - 1 - lax.broadcasted_iota(jnp.int32, (SUB, LANES), 1)
    chunks = range(0, values.shape[-1], LANES)
    parts = [jnp.take_along_axis(values[:, c : c + LANES], index, axis=1) for c in reversed(chunks)]
    return jnp.concatenate(parts, axis=1)


def run_copies(copies):
    for copy in copies:
        copy.start()
    for copy in copies:
        copy.wait()


def columns_kernel(vel, thick, trac, mask, out_a, out_b, edges, land, sem):
    levels, rows, width = thick.shape
    half_rows = rows // 2
    copies = []
    for side in range(2):
        lanes = pl.ds(side * (width - LANES), LANES)
        to = pl.ds(side * LANES, LANES)
        for level in range(levels):
            for half in range(2):
                at, s = pl.ds(half * half_rows, half_rows), 2 * level + half
                for source, target in (
                    (vel.at[:, level, at, lanes], edges.at[0:2, :, s, to]),
                    (thick.at[level, at, lanes], edges.at[2, :, s, to]),
                    (trac.at[:, level, at, lanes], edges.at[3:5, :, s, to]),
                    (mask.at[level, at, lanes], land.at[:, s, to]),
                ):
                    copies.append(pltpu.make_async_copy(source, target, sem))
    run_copies(copies)
    lon_even = lax.axis_index("lon") % 2 == 0
    group = lax.broadcasted_iota(jnp.int32, (SUB, LANES), 1) // HALO
    for f in range(6):
        west = east = jnp.zeros((SUB, LANES), F32)
        for row in range(half_rows):
            pair = edges[f, row] if f < 5 else HYPERVISCOSITY * land[row].astype(F32)
            here = group == row
            west = jnp.where(here, pltpu.roll(pair[:, :LANES], HALO * row % LANES, 1), west)
            east = jnp.where(here, pltpu.roll(pair[:, LANES:], HALO * (row + 1) % LANES, 1), east)
        out_a[f] = jnp.where(lon_even, east, west)
        out_b[f] = jnp.where(lon_even, west, east)


def load_kernel(lat_count, vel, thick, trac, mask, after, planes, coriolis, land, sem):
    del after
    levels, rows, width = thick.shape
    half_rows = rows // 2
    length = half_rows + PAD
    copies = []
    for level in range(levels):
        for half in range(2):
            at, s = pl.ds(half * (half_rows - PAD), length), 2 * level + half
            to = pl.ds((1 - half) * PAD, length)
            for source, target in (
                (vel.at[:, level, at, :], planes.at[0:2, to, s, :]),
                (thick.at[level, at, :], planes.at[2, to, s, :]),
                (trac.at[:, level, at, :], planes.at[3:5, to, s, :]),
                (mask.at[level, at, :], land.at[to, s, :]),
            ):
                copies.append(pltpu.make_async_copy(source, target, sem))
    for copy in copies:
        copy.start()
    total = rows * lat_count
    half = lax.broadcasted_iota(jnp.int32, (SUB, LANES), 0) % 2
    first = lax.axis_index("lat") * rows + half * half_rows
    for row in range(-2, half_rows + 2):
        ids = first + row
        folded = jnp.where(ids >= total, 2 * total - 1 - ids, ids)
        angle = jnp.pi * (folded.astype(F32) + 0.5) / total - jnp.pi / 2
        coriolis[row + PAD] = (CORIOLIS / HYPERVISCOSITY) * jnp.sin(angle)
    for copy in copies:
        copy.wait()
    for row in range(PAD - 2, half_rows + PAD + 2):
        planes[5, row] = HYPERVISCOSITY * land[row].astype(F32)


def halo_columns(cols_a, cols_b, lon_even):
    lane = lax.broadcasted_iota(jnp.int32, (SUB, LANES), 1)

    def get(f):
        a, b = cols_a[f], cols_b[f]
        from_west = jnp.where(lon_even, b, a)
        from_east = jnp.where(lon_even, a, b)

        def row(r):
            east = pltpu.roll(from_east, -HALO * r % LANES, 1)
            west = pltpu.roll(from_west, -HALO * (r + 1) % LANES, 1)
            return jnp.where(lane < LANES // 2, east, west)

        return row

    return get


def rows_kernel(lat_count, planes, cols_a, cols_b, out_a, out_b):
    half_rows, width = planes.shape[1] - 2 * PAD, planes.shape[3]
    chunks = width // LANES
    lat = lax.axis_index("lat")
    lat_even = lat % 2 == 0
    lon_even = lax.axis_index("lon") % 2 == 0
    even = even_half(width + LANES)
    group = lax.broadcasted_iota(jnp.int32, (SUB, LANES), 1) // 8
    get = halo_columns(cols_a, cols_b, lon_even)
    column = [get(f) for f in range(6)]
    slots = [(f, m) for f in range(5) for m in range(2)] + [(5, None)]

    def whole(f, row):
        return jnp.concatenate([planes[f, row + PAD], column[f](row)], axis=1)

    def north(f, m):
        low = half_rows - HALO + 2 * m
        return jnp.where(even, pltpu.roll(whole(f, low + 1), SUB - 1, 0), whole(f, low))

    def south(f, m):
        return jnp.where(even, whole(f, 2 * m), pltpu.roll(whole(f, 2 * m + 1), 1, 0))

    def put(target, slot, value):
        for c in range(chunks):
            target[chunks * slot + c] = value[:, c * LANES : (c + 1) * LANES]

    def add_corner(corner, slot, value):
        return jnp.where(group == slot, pltpu.roll(value[:, width:], 8 * slot + HALO, 1), corner)

    corner_a = corner_b = jnp.zeros((SUB, LANES), F32)
    for slot, (f, m) in enumerate(slots):
        to_north = north(f, 1 if m is None else m)
        to_south = south(f, 0 if m is None else m)
        a = jnp.where(lat_even, to_north, to_south)
        b = jnp.where(lat_even, to_south, to_north)
        put(out_a, slot, a)
        put(out_b, slot, b)
        corner_a = add_corner(corner_a, slot, a)
        corner_b = add_corner(corner_b, slot, b)
    out_a[chunks * SLOTS] = corner_a
    out_b[chunks * SLOTS] = corner_b

    @pl.when(lat == lat_count - 1)
    def _():
        target = out_a if (lat_count - 1) % 2 == 0 else out_b
        corner = jnp.zeros((SUB, LANES), F32)
        for slot, (f, m) in enumerate(slots):
            value = north(f, 1 if m is None else 1 - m)
            value = -value if f < 2 else value
            mirrored = jnp.concatenate([flip_lanes(value[:, :width]), flip_lanes(value[:, width:])], axis=1)
            put(target, slot, mirrored)
            corner = add_corner(corner, slot, mirrored)
        target[chunks * SLOTS] = corner


def make_step(wide, sums, east_diff, press):
    scale = 1.0 / HYPERVISCOSITY
    keep_own = scale * (1.0 - 4.0 * DIFFUSION - 16.0 * HYPERVISCOSITY)
    keep_sum = scale * (DIFFUSION + 8.0 * HYPERVISCOSITY)
    advect = -0.5 * ADVECTION * scale
    slope = -0.5 * GRADIENT * scale
    converge = -0.5 * CONVERGENCE * scale
    level = lax.broadcasted_iota(jnp.int32, (SUB, wide), 0) // 2
    weight = slope / (level.astype(F32) + 1.0)
    below_one, below_two = level >= 1, level >= 2

    def shifts(value):
        return pltpu.roll(value, wide - 1, 1), pltpu.roll(value, 1, 1)

    def ahead(source, row, at, f):
        to_east, to_west = shifts(source(f, row))
        sums[f, at] = (to_east + to_west) + (source(f, row + 1) + source(f, row - 1))
        east_diff[f, at] = to_east - to_west

    def ahead_press(source, row, at):
        part = weight * source(2, row) + ((0.08 * slope) * source(4, row) - (0.1 * slope) * source(3, row))
        part = part + jnp.where(below_one, pltpu.roll(part, 2, 0), 0.0)
        press[at] = part + jnp.where(below_two, pltpu.roll(part, 4, 0), 0.0)

    def update(source, ocean, turn, row, at, cut, emit, northward):
        lanes = slice(0, cut)
        turn = jnp.concatenate([turn] * (cut // LANES), axis=1)
        u, v = source(0, row)[:, lanes], source(1, row)[:, lanes]
        along_u, along_v = advect * u, advect * v
        if northward is not None:
            along_v = along_v * northward[:, lanes]

        def add_on(f):
            if f == 0:
                p_east, p_west = shifts(press[at])
                return turn * v + (p_east - p_west)[:, lanes]
            if f == 1:
                rise = press[at + 1, :, lanes] - press[at - 1, :, lanes]
                if northward is not None:
                    rise = rise * northward[:, lanes]
                return rise - turn * u
            v_north = source(1, row + 1)[:, lanes] - source(1, row - 1)[:, lanes]
            if northward is not None:
                v_north = v_north * northward[:, lanes]
            return converge * (east_diff[0, at, :, lanes] + v_north)

        def one(f):
            here = sums[f, at]
            s_east, s_west = shifts(here)
            around = (s_east + s_west)[:, lanes] + (sums[f, at + 1, :, lanes] + sums[f, at - 1, :, lanes])
            dx = east_diff[f, at, :, lanes]
            dy = source(f, row + 1)[:, lanes] - source(f, row - 1)[:, lanes]
            value = keep_own * source(f, row)[:, lanes] + (keep_sum * here[:, lanes] - around)
            value = value + (along_u * dx + along_v * dy)
            if f < 3:
                value = value + add_on(f)
            emit(f, row, value * ocean)

        return one

    def advance(source, ocean, turn, row, at, cut, emit, northward=None):
        ahead_press(source, row + 1, at + 1)
        one = None
        for f in range(5):
            ahead(source, row + 1, at + 1, f)
            one = one or update(source, ocean(), turn(), row, at, cut, emit, northward)
            one(f)

    def begin(source, rows, ats):
        for row, at in zip(rows, ats):
            ahead_press(source, row, at)
            for f in range(5):
                ahead(source, row, at, f)

    return begin, advance


def swap_halves(value):
    even = even_half(value.shape[-1])
    return jnp.where(even, pltpu.roll(value, SUB - 1, 0), pltpu.roll(value, 1, 0))


def interior_kernel(
    planes, cols_a, cols_b, coriolis, after, out, middle, joint, ring, outer, second, centre, sums, east_diff, press
):
    del after
    half_rows, width = planes.shape[1] - 2 * PAD, planes.shape[3]
    last = half_rows - 1
    wide = width + LANES
    lon_even = lax.axis_index("lon") % 2 == 0
    get = halo_columns(cols_a, cols_b, lon_even)
    for f in range(6):
        column = get(f)
        for row in range(half_rows):
            value = column(row)
            outer[f, row + PAD] = value
            if row < HALO:
                outer[f, row + PAD + half_rows] = pltpu.roll(value, SUB - 1, 0)
            if row >= half_rows - HALO:
                outer[f, row + PAD - half_rows] = pltpu.roll(value, 1, 0)
    begin, advance = make_step(wide, sums, east_diff, press)
    even = even_half(wide)

    def whole(f, row):
        return jnp.concatenate([planes[f, row + PAD], outer[f, row + PAD]], axis=1)

    def keep(f, row, value):
        second[f, row + PAD] = value

    def halfway(f, row):
        return second[f, row + PAD]

    def write(f, row, value):
        out[f, row] = value

    def sweep(source, low, high, cut, emit):
        begin(source, (low - 1, low), (low - 1 + PAD, low + PAD))

        def iteration(row, carry):
            ocean = lambda: whole(5, row)[:, :cut]
            turn = lambda: coriolis[row + PAD]
            advance(source, ocean, turn, row, row + PAD, cut, emit)
            return carry

        lax.fori_loop(low, high, iteration, 0, unroll=4)

    sweep(whole, 2, half_rows - 2, wide, keep)

    for i in range(4):
        for f in range(6):
            joint[f, i] = jnp.where(even, whole(f, i), whole(f, last - i))
        for f in range(5):
            ring[f, i] = jnp.where(even, halfway(f, 2 + i), halfway(f, last - 2 - i))

    def mirrored(f, i):
        return jnp.where(even, whole(f, last - i), whole(f, i))

    north_odd = jnp.where(even, -1.0, 1.0)
    ocean_of = lambda i, cut: lambda: mirrored(5, i)[:, :cut]
    turn_of = lambda i: lambda: jnp.where(even[:, :LANES], coriolis[last - i + PAD], coriolis[i + PAD])

    def keep_centre(f, i, value):
        centre[f, i + 2] = value
        centre[f, 1 - i] = swap_halves(value)

    begin(mirrored, (-1, 0), (0, 1))
    for i in range(2):
        advance(mirrored, ocean_of(i, wide), turn_of(i), i, i + 1, wide, keep_centre, north_odd)

    def centre_halfway(f, i):
        return centre[f, i + 2] if i < 2 else jnp.where(even, halfway(f, last - i), halfway(f, i))

    def keep_middle(f, i, value):
        middle[f, i] = value

    begin(centre_halfway, (-1, 0), (0, 1))
    for i in range(4):
        advance(centre_halfway, ocean_of(i, width), turn_of(i), i, i + 1, width, keep_middle, north_odd)

    sweep(halfway, HALO, half_rows - HALO, width, write)


def edges_kernel(
    joint, ring, middle, coriolis, done, rows_a, rows_b, vel_out, thick_out, trac_out, strip, first, second, sums, east_diff, press, sem
):
    half_rows, width = done.shape[1], done.shape[3]
    wide = width + LANES
    chunks = width // LANES
    levels = SUB // 2

    def copies_out(source, source_row, row, count):
        copies = []
        for level in range(levels):
            for half in range(2):
                s = 2 * level + half
                rows, to = pl.ds(source_row, count), pl.ds(half * half_rows + row, count)
                copies += [
                    pltpu.make_async_copy(source.at[0:2, rows, s, :], vel_out.at[:, level, to, :], sem),
                    pltpu.make_async_copy(source.at[2, rows, s, :], thick_out.at[level, to, :], sem),
                    pltpu.make_async_copy(source.at[3:5, rows, s, :], trac_out.at[:, level, to, :], sem),
                ]
        for copy in copies:
            copy.start()
        return copies

    copies = copies_out(done, PAD, PAD, half_rows - 2 * PAD)
    for f in range(5):
        for i in range(HALO):
            strip[f, HALO + i] = done[f, HALO + i]
            strip[f, PAD + i] = done[f, half_rows - PAD + i]
    lat = lax.axis_index("lat")
    lat_even, southmost = lat % 2 == 0, lat == 0
    even, even_one = even_half(wide), even_half(LANES)
    even_out = even_half(width)
    corner_a, corner_b = rows_a[chunks * SLOTS], rows_b[chunks * SLOTS]

    def message(ref, corner, slot):
        parts = [ref[chunks * slot + c] for c in range(chunks)]
        return jnp.concatenate([*parts, pltpu.roll(corner, -(8 * slot + HALO) % LANES, 1)], axis=1)

    for f in range(6):
        reach = HALO if f < 5 else 2
        for m in range(reach // 2):
            slot, opposite = 2 * f + m, 2 * f + reach // 2 - 1 - m
            south = [message(ref, corner, slot) for ref, corner in ((rows_a, corner_a), (rows_b, corner_b))]
            north = [message(ref, corner, opposite) for ref, corner in ((rows_a, corner_a), (rows_b, corner_b))]
            from_south = jnp.where(southmost, 0.0, jnp.where(lat_even, south[1], south[0]))
            from_north = jnp.where(lat_even, north[0], north[1])
            row = 2 * m - reach
            first[f, row + HALO] = jnp.where(even, pltpu.roll(from_south, SUB - 1, 0), from_north)
            first[f, row + 1 + HALO] = jnp.where(even, from_south, pltpu.roll(from_north, 1, 0))

    def whole(f, i):
        return first[f, i + HALO] if i < 0 else joint[f, i]

    def halfway(f, i):
        return second[f, i + 2] if i < 2 else ring[f, i - 2]

    def keep(f, i, value):
        second[f, i + 2] = value

    def write(f, i, value):
        other = middle[f, i]
        strip[f, i] = jnp.where(even_out, value, other)
        strip[f, 2 * PAD - 1 - i] = jnp.where(even_out, other, value)

    begin, advance = make_step(wide, sums, east_diff, press)
    north_even = jnp.where(even, 1.0, -1.0)

    def sweep(source, low, high, cut, emit):
        begin(source, (low - 1, low), (low + 3, low + 4))
        for i in range(low, high):
            ocean = lambda: whole(5, i)[:, :cut]
            turn = lambda: jnp.where(even_one, coriolis[i + PAD], coriolis[half_rows - 1 - i + PAD])
            advance(source, ocean, turn, i, i + 4, cut, emit, north_even)

    sweep(whole, -2, 2, wide, keep)
    sweep(halfway, 0, HALO, width, write)
    copies += copies_out(strip, 0, 0, PAD)
    copies += copies_out(strip, PAD, half_rows - PAD, PAD)
    for copy in copies:
        copy.wait()


def lat_pairs(parity, lat_count, lon_count):
    pairs = []
    for lat in range(lat_count):
        for lon in range(lon_count):
            to_lat, to_lon = (lat + 1 if lat % 2 == parity else lat - 1), lon
            if to_lat < 0:
                to_lat, to_lon = 0, lon ^ 1
            if to_lat == lat_count:
                to_lat, to_lon = lat, lon_count - 1 - lon
            pairs.append((lon * lat_count + lat, to_lon * lat_count + to_lat))
    return pairs


def lon_pairs(parity, lon_count):
    return [(i, (i + 1 if i % 2 == parity else i - 1) % lon_count) for i in range(lon_count)]


def shapes(*dims):
    return jax.ShapeDtypeStruct(dims, F32)


def body(lat_count, lon_count, velocity, thickness, tracers, land_mask):
    levels, rows, width = thickness.shape
    half_rows = rows // 2
    wide, tall = width + LANES, half_rows + 2 * PAD
    arguments = (velocity, thickness, tracers, land_mask)
    fields = [pltpu.with_memory_space_constraint(x, pltpu.HBM) for x in arguments]
    dma = pltpu.SemaphoreType.DMA

    def call(kernel, name, in_specs, outs, out_specs, scratch, flops):
        return pl.pallas_call(
            kernel,
            out_shape=outs,
            in_specs=in_specs,
            out_specs=out_specs,
            scratch_shapes=scratch,
            compiler_params=pltpu.CompilerParams(vmem_limit_bytes=40 * 2**20),
            cost_estimate=pl.CostEstimate(flops=flops, bytes_accessed=flops // 10, transcendentals=0),
            name=name,
        )

    columns = shapes(6, SUB, LANES)
    send_a, send_b = call(
        columns_kernel,
        "pack_columns",
        [HBM] * 4,
        (columns, columns),
        (VMEM, VMEM),
        [pltpu.VMEM((5, half_rows, SUB, 2 * LANES), F32), pltpu.VMEM((half_rows, SUB, 2 * LANES), jnp.int32), dma],
        10**6,
    )(*fields)
    cols_a = lax.ppermute(send_a, "lon", lon_pairs(0, lon_count))
    cols_b = lax.ppermute(send_b, "lon", lon_pairs(1, lon_count))

    planes, coriolis = call(
        functools.partial(load_kernel, lat_count),
        "load_fields",
        [HBM, HBM, HBM, HBM, ANY],
        (shapes(6, tall, SUB, width), shapes(tall, SUB, LANES)),
        (VMEM, VMEM),
        [pltpu.VMEM((tall, SUB, width), jnp.int32), dma],
        10**8,
    )(*fields, send_a)

    message = shapes(SLOTS * (width // LANES) + 1, SUB, LANES)
    send_a, send_b = call(
        functools.partial(rows_kernel, lat_count),
        "pack_rows",
        [VMEM] * 3,
        (message, message),
        (VMEM, VMEM),
        [],
        10**6,
    )(planes, cols_a, cols_b)
    axes = ("lon", "lat")
    rows_a = lax.ppermute(send_a, axes, lat_pairs(0, lat_count, lon_count))
    rows_b = lax.ppermute(send_b, axes, lat_pairs(1, lat_count, lon_count))

    def work(length):
        tall_planes = pltpu.VMEM((5, length, SUB, wide), F32)
        return [tall_planes, tall_planes, pltpu.VMEM((length, SUB, wide), F32)]

    done, middle, joint, ring = call(
        interior_kernel,
        "interior",
        [VMEM, VMEM, VMEM, VMEM, ANY],
        (
            shapes(5, half_rows, SUB, width),
            shapes(5, 4, SUB, width),
            shapes(6, 4, SUB, wide),
            shapes(5, 4, SUB, wide),
        ),
        (VMEM, VMEM, VMEM, VMEM),
        [
            pltpu.VMEM((6, tall, SUB, LANES), F32),
            pltpu.VMEM((5, tall, SUB, wide), F32),
            pltpu.VMEM((5, 4, SUB, wide), F32),
            *work(tall),
        ],
        10**8,
    )(planes, cols_a, cols_b, coriolis, send_a)

    return call(
        edges_kernel,
        "edges",
        [VMEM] * 7,
        (shapes(*velocity.shape), shapes(*thickness.shape), shapes(*tracers.shape)),
        (HBM, HBM, HBM),
        [
            pltpu.VMEM((5, 2 * PAD, SUB, width), F32),
            pltpu.VMEM((6, HALO, SUB, wide), F32),
            pltpu.VMEM((5, 4, SUB, wide), F32),
            *work(10),
            dma,
        ],
        10**8,
    )(joint, ring, middle, coriolis, done, rows_a, rows_b)


def solution(mesh):
    specs = (P(None, None, "lat", "lon"), P(None, "lat", "lon"), P(None, None, "lat", "lon"))
    return jax.shard_map(
        functools.partial(body, mesh.shape["lat"], mesh.shape["lon"]),
        mesh=mesh,
        in_specs=(*specs, P(None, "lat", "lon")),
        out_specs=specs,
        check_vma=False,
    )
```

```python
import functools

import jax
import jax.numpy as jnp
from jax import lax
from jax.experimental import pallas as pl
from jax.experimental.pallas import tpu as pltpu
from jax.sharding import PartitionSpec as P

ADVECTION = 0.25
DIFFUSION = 0.05
HYPERVISCOSITY = 0.02
CORIOLIS = 0.3
GRADIENT = 0.2
CONVERGENCE = 0.3

HALO = 4
PAD = 8
LANES = 128
SUB = 8
SLOTS = 11
ROLLED = 4
F32 = jnp.float32
VMEM = pl.BlockSpec(memory_space=pltpu.VMEM)
HBM = pl.BlockSpec(memory_space=pltpu.HBM)
ANY = pl.BlockSpec(memory_space=pl.ANY)


def even_half(lanes):
    return lax.broadcasted_iota(jnp.int32, (SUB, lanes), 0) % 2 == 0


def flip_lanes(values):
    index = LANES - 1 - lax.broadcasted_iota(jnp.int32, (SUB, LANES), 1)
    chunks = range(0, values.shape[-1], LANES)
    parts = [jnp.take_along_axis(values[:, c : c + LANES], index, axis=1) for c in reversed(chunks)]
    return jnp.concatenate(parts, axis=1)


def columns_kernel(vel, thick, trac, mask, out_a, out_b, edges, land, sem):
    levels, rows, width = thick.shape
    half_rows = rows // 2
    groups = {0: [], 2: [], 3: [], 5: []}
    for side in range(2):
        lanes = pl.ds(side * (width - LANES), LANES)
        to = pl.ds(side * LANES, LANES)
        for level in range(levels):
            for half in range(2):
                at, s = pl.ds(half * half_rows, half_rows), 2 * level + half
                for f, source, target in (
                    (0, vel.at[:, level, at, lanes], edges.at[0:2, :, s, to]),
                    (2, thick.at[level, at, lanes], edges.at[2, :, s, to]),
                    (3, trac.at[:, level, at, lanes], edges.at[3:5, :, s, to]),
                    (5, mask.at[level, at, lanes], land.at[:, s, to]),
                ):
                    groups[f].append(pltpu.make_async_copy(source, target, sem.at[f]))
    for f in groups:
        for copy in groups[f]:
            copy.start()
    lon_even = lax.axis_index("lon") % 2 == 0
    group = lax.broadcasted_iota(jnp.int32, (SUB, LANES), 1) // HALO
    for f in range(6):
        for copy in groups.get(f, ()):
            copy.wait()
        west = east = jnp.zeros((SUB, LANES), F32)
        for row in range(half_rows):
            pair = edges[f, row] if f < 5 else HYPERVISCOSITY * land[row].astype(F32)
            here = group == row
            west = jnp.where(here, pltpu.roll(pair[:, :LANES], HALO * row % LANES, 1), west)
            east = jnp.where(here, pltpu.roll(pair[:, LANES:], HALO * (row + 1) % LANES, 1), east)
        out_a[f] = jnp.where(lon_even, east, west)
        out_b[f] = jnp.where(lon_even, west, east)


def load_kernel(lat_count, vel, thick, trac, mask, after, planes, from_east, from_west, coriolis, land, sem):
    del after
    levels, rows, width = thick.shape
    half_rows = rows // 2
    length = half_rows + PAD
    groups = {0: [], 2: [], 3: [], 5: []}
    for level in range(levels):
        for half in range(2):
            at, s = pl.ds(half * (half_rows - PAD), length), 2 * level + half
            to = pl.ds((1 - half) * PAD, length)
            for f, source, target in (
                (0, vel.at[:, level, at, :], planes.at[0:2, to, s, :]),
                (2, thick.at[level, at, :], planes.at[2, to, s, :]),
                (3, trac.at[:, level, at, :], planes.at[3:5, to, s, :]),
                (5, mask.at[level, at, :], land.at[to, s, :]),
            ):
                groups[f].append(pltpu.make_async_copy(source, target, sem.at[f]))
    for f in groups:
        for copy in groups[f]:
            copy.start()
    total = rows * lat_count
    half = lax.broadcasted_iota(jnp.int32, (SUB, LANES), 0) % 2
    first = lax.axis_index("lat") * rows + half * half_rows
    for row in range(-2, half_rows + 2):
        ids = first + row
        folded = jnp.where(ids >= total, 2 * total - 1 - ids, ids)
        angle = jnp.pi * (folded.astype(F32) + 0.5) / total - jnp.pi / 2
        coriolis[row + PAD] = (CORIOLIS / HYPERVISCOSITY) * jnp.sin(angle)
    for f in range(6):
        for copy in groups.get(f, ()):
            copy.wait()
        if f == 5:
            break
        for row in range(PAD, half_rows + PAD) if f < ROLLED else ():
            value = planes[f, row]
            from_east[f, row] = pltpu.roll(value, width - 1, 1)
            from_west[f, row] = pltpu.roll(value, 1, 1)
    for row in range(PAD - 2, half_rows + PAD + 2):
        planes[5, row] = HYPERVISCOSITY * land[row].astype(F32)


def halo_columns(cols_a, cols_b, lon_even):
    def get(f):
        a, b = cols_a[f], cols_b[f]
        return halo_of(jnp.where(lon_even, a, b), jnp.where(lon_even, b, a))

    return get


def halo_of(from_east, from_west):
    lane = lax.broadcasted_iota(jnp.int32, (SUB, LANES), 1)

    def row(r):
        east = pltpu.roll(from_east, (LANES - HALO * r) % LANES, 1)
        west = pltpu.roll(from_west, LANES - HALO * (r + 1), 1)
        return jnp.where(lane < LANES // 2, east, west)

    return row


def rows_kernel(lat_count, planes, cols_a, cols_b, out_a, out_b):
    half_rows, width = planes.shape[1] - 2 * PAD, planes.shape[3]
    chunks = width // LANES
    lat = lax.axis_index("lat")
    lat_even = lat % 2 == 0
    lon_even = lax.axis_index("lon") % 2 == 0
    even = even_half(width + LANES)
    group = lax.broadcasted_iota(jnp.int32, (SUB, LANES), 1) // 8
    get = halo_columns(cols_a, cols_b, lon_even)
    column = [get(f) for f in range(6)]
    slots = [(f, m) for f in range(5) for m in range(2)] + [(5, None)]

    def whole(f, row):
        return jnp.concatenate([planes[f, row + PAD], column[f](row)], axis=1)

    def north(f, m):
        low = half_rows - HALO + 2 * m
        return jnp.where(even, pltpu.roll(whole(f, low + 1), SUB - 1, 0), whole(f, low))

    def south(f, m):
        return jnp.where(even, whole(f, 2 * m), pltpu.roll(whole(f, 2 * m + 1), 1, 0))

    def put(target, slot, value):
        for c in range(chunks):
            target[chunks * slot + c] = value[:, c * LANES : (c + 1) * LANES]

    def add_corner(corner, slot, value):
        return jnp.where(group == slot, pltpu.roll(value[:, width:], 8 * slot + HALO, 1), corner)

    corner_a = corner_b = jnp.zeros((SUB, LANES), F32)
    for slot, (f, m) in enumerate(slots):
        to_north = north(f, 1 if m is None else m)
        to_south = south(f, 0 if m is None else m)
        a = jnp.where(lat_even, to_north, to_south)
        b = jnp.where(lat_even, to_south, to_north)
        put(out_a, slot, a)
        put(out_b, slot, b)
        corner_a = add_corner(corner_a, slot, a)
        corner_b = add_corner(corner_b, slot, b)
    out_a[chunks * SLOTS] = corner_a
    out_b[chunks * SLOTS] = corner_b

    @pl.when(lat == lat_count - 1)
    def _():
        target = out_a if (lat_count - 1) % 2 == 0 else out_b
        corner = jnp.zeros((SUB, LANES), F32)
        for slot, (f, m) in enumerate(slots):
            value = north(f, 1 if m is None else 1 - m)
            value = -value if f < 2 else value
            mirrored = jnp.concatenate([flip_lanes(value[:, :width]), flip_lanes(value[:, width:])], axis=1)
            put(target, slot, mirrored)
            corner = add_corner(corner, slot, mirrored)
        target[chunks * SLOTS] = corner


def make_step(wide, sums, east_diff, press):
    scale = 1.0 / HYPERVISCOSITY
    keep_own = scale * (1.0 - 4.0 * DIFFUSION - 16.0 * HYPERVISCOSITY)
    keep_sum = scale * (DIFFUSION + 8.0 * HYPERVISCOSITY)
    advect = -0.5 * ADVECTION * scale
    slope = -0.5 * GRADIENT * scale
    converge = -0.5 * CONVERGENCE * scale
    level = lax.broadcasted_iota(jnp.int32, (SUB, wide), 0) // 2
    weight = slope / (level.astype(F32) + 1.0)
    below_one, below_two = level >= 1, level >= 2

    def shifts(value):
        return pltpu.roll(value, wide - 1, 1), pltpu.roll(value, 1, 1)

    def ahead(source, row, at, f, shifted):
        to_east, to_west = shifted(f, row) if shifted else shifts(source(f, row))
        sums[f, at] = (to_east + to_west) + (source(f, row + 1) + source(f, row - 1))
        east_diff[f, at] = to_east - to_west

    def weighed_down(thick, temp, salt):
        lanes = slice(0, thick.shape[-1])
        part = weight[:, lanes] * thick + ((0.08 * slope) * salt - (0.1 * slope) * temp)
        part = part + jnp.where(below_one[:, lanes], pltpu.roll(part, 2, 0), 0.0)
        return part + jnp.where(below_two[:, lanes], pltpu.roll(part, 4, 0), 0.0)

    def ahead_press(source, row, at):
        press[at] = weighed_down(source(2, row), source(3, row), source(4, row))

    def update_row(source, ocean, turn, row, at, cut, emit, northward=None, roll_press=False):
        lanes = slice(0, cut)
        turn = jnp.concatenate([turn] * (cut // LANES), axis=1)
        u, v = source(0, row)[:, lanes], source(1, row)[:, lanes]
        along_u, along_v = advect * u, advect * v
        if northward is not None:
            along_v = along_v * northward[:, lanes]

        def add_on(f):
            if f == 0:
                if roll_press:
                    p_east, p_west = shifts(press[at])
                    return turn * v + (p_east - p_west)[:, lanes]
                slopes = [east_diff[field, at, :, lanes] for field in (2, 3, 4)]
                return turn * v + weighed_down(*slopes)
            if f == 1:
                rise = press[at + 1, :, lanes] - press[at - 1, :, lanes]
                if northward is not None:
                    rise = rise * northward[:, lanes]
                return rise - turn * u
            v_north = source(1, row + 1)[:, lanes] - source(1, row - 1)[:, lanes]
            if northward is not None:
                v_north = v_north * northward[:, lanes]
            return converge * (east_diff[0, at, :, lanes] + v_north)

        def one(f):
            here = sums[f, at]
            s_east, s_west = shifts(here)
            around = (s_east + s_west)[:, lanes] + (sums[f, at + 1, :, lanes] + sums[f, at - 1, :, lanes])
            dx = east_diff[f, at, :, lanes]
            dy = source(f, row + 1)[:, lanes] - source(f, row - 1)[:, lanes]
            value = keep_own * source(f, row)[:, lanes] + (keep_sum * here[:, lanes] - around)
            value = value + (along_u * dx + along_v * dy)
            if f < 3:
                value = value + add_on(f)
            emit(f, row, value * ocean)

        for f in range(5):
            one(f)

    def ahead_row(source, row, at, shifted=None):
        ahead_press(source, row, at)
        for f in range(5):
            ahead(source, row, at, f, shifted)

    return ahead_row, update_row


def swap_halves(value):
    even = even_half(value.shape[-1])
    return jnp.where(even, pltpu.roll(value, SUB - 1, 0), pltpu.roll(value, 1, 0))


def interior_kernel(
    planes,
    from_east,
    from_west,
    cols_a,
    cols_b,
    coriolis,
    after,
    out,
    middle,
    joint,
    ring,
    joint_sums,
    joint_diff,
    joint_press,
    outer,
    sides,
    second,
    centre,
    sums,
    east_diff,
    press,
):
    del after
    half_rows, width = planes.shape[1] - 2 * PAD, planes.shape[3]
    last = half_rows - 1
    wide = width + LANES
    lon_even = lax.axis_index("lon") % 2 == 0
    for f in range(6):
        a, b = cols_a[f], cols_b[f]
        sides[0, f] = jnp.where(lon_even, a, b)
        sides[1, f] = jnp.where(lon_even, b, a)

    def add_halo(row):
        for f in range(6):
            outer[f, row + PAD] = halo_of(sides[0, f], sides[1, f])(row)

    for row in range(4):
        add_halo(row)
    ahead_row, update_row = make_step(wide, sums, east_diff, press)
    even = even_half(wide)
    lane = lax.broadcasted_iota(jnp.int32, (SUB, LANES), 1)
    at_first, at_last = lane == 0, lane == LANES - 1

    def whole(f, row):
        return jnp.concatenate([planes[f, row + PAD], outer[f, row + PAD]], axis=1)

    def whole_shifted(f, row):
        at = row + PAD
        if f >= ROLLED:
            return pltpu.roll(whole(f, row), wide - 1, 1), pltpu.roll(whole(f, row), 1, 1)
        east, west, halo = from_east[f, at], from_west[f, at], outer[f, at]
        halo_east, halo_west = pltpu.roll(halo, LANES - 1, 1), pltpu.roll(halo, 1, 1)
        tail, head = east[:, width - LANES :], west[:, :LANES]
        east = [east[:, : width - LANES], jnp.where(at_last, halo_east, tail), jnp.where(at_last, tail, halo_east)]
        west = [jnp.where(at_first, halo_west, head), west[:, LANES:], jnp.where(at_first, head, halo_west)]
        return jnp.concatenate(east, axis=1), jnp.concatenate(west, axis=1)

    def keep(f, row, value):
        second[f, row + PAD] = value

    def halfway(f, row):
        return second[f, row + PAD]

    def write(f, row, value):
        out[f, row] = value

    def sweep(source, low, high, cut, emit, shifted=None):
        ahead_row(source, low - 1, low - 1 + PAD, shifted)
        ahead_row(source, low, low + PAD, shifted)

        def iteration(row, carry):
            if shifted:
                add_halo(row + 2)
            ahead_row(source, row + 1, row + 1 + PAD, shifted)
            ocean, turn = whole(5, row)[:, :cut], coriolis[row + PAD]
            update_row(source, ocean, turn, row, row + PAD, cut, emit, roll_press=bool(shifted))
            return carry

        lax.fori_loop(low, high, iteration, 0, unroll=(high - low) // 2)

    def outer_pair(ref, i):
        return jnp.where(even, ref[i + PAD], ref[last - i + PAD])

    def inner_pair(ref, i):
        return jnp.where(even, ref[last - i + PAD], ref[i + PAD])

    def save_outer(step, i):
        for f in range(5):
            for k in range(2):
                joint_sums[step, f, k] = outer_pair(sums.at[f], i + k)
            joint_diff[step, f] = outer_pair(east_diff.at[f], i)
        for k in range(2):
            joint_press[step, k] = outer_pair(press, i + k)

    def take_inner(i):
        for f in range(5):
            sums[f, i + 1] = inner_pair(sums.at[f], i)
            east_diff[f, i + 1] = inner_pair(east_diff.at[f], i)
        press[i + 1] = inner_pair(press, i)

    def fold_inner():
        for f in range(5):
            sums[f, 0] = swap_halves(sums[f, 1])
        press[0] = swap_halves(press[1])

    sweep(whole, 2, half_rows - 2, wide, keep, whole_shifted)
    for f in range(5):
        outer[f, half_rows + PAD] = pltpu.roll(outer[f, PAD], SUB - 1, 0)
        outer[f, PAD - 1] = pltpu.roll(outer[f, last + PAD], 1, 0)
    save_outer(0, 1)
    for i in range(4):
        for f in range(6):
            joint[f, i] = jnp.where(even, whole(f, i), whole(f, last - i))
        for f in range(5):
            ring[f, i] = outer_pair(second.at[f], 2 + i)

    def mirrored(f, i):
        return jnp.where(even, whole(f, last - i), whole(f, i))

    def mirrored_shifted(f, i):
        south, north = whole_shifted(f, last - i), whole_shifted(f, i)
        return [jnp.where(even, one, other) for one, other in zip(south, north)]

    north_odd = jnp.where(even, -1.0, 1.0)

    def turn_of(i):
        return jnp.where(even[:, :LANES], coriolis[last - i + PAD], coriolis[i + PAD])

    def keep_centre(f, i, value):
        centre[f, i + 2] = value
        centre[f, 1 - i] = swap_halves(value)

    ahead_row(mirrored, 0, 1, mirrored_shifted)
    fold_inner()
    take_inner(1)
    take_inner(2)
    for i in range(2):
        update_row(mirrored, mirrored(5, i), turn_of(i), i, i + 1, wide, keep_centre, north_odd)

    sweep(halfway, HALO, half_rows - HALO, width, write)
    save_outer(1, 3)

    def centre_halfway(f, i):
        return centre[f, i + 2] if i < 2 else inner_pair(second.at[f], i)

    def keep_middle(f, i, value):
        middle[f, i] = value

    for i in range(3):
        ahead_row(centre_halfway, i, i + 1)
    fold_inner()
    take_inner(3)
    take_inner(4)
    for i in range(4):
        ocean = mirrored(5, i)[:, :width]
        update_row(centre_halfway, ocean, turn_of(i), i, i + 1, width, keep_middle, north_odd)


def edges_kernel(
    joint,
    ring,
    joint_sums,
    joint_diff,
    joint_press,
    middle,
    coriolis,
    done,
    rows_a,
    rows_b,
    vel_out,
    thick_out,
    trac_out,
    strip,
    first,
    second,
    sums,
    east_diff,
    press,
    sem,
):
    half_rows, width = done.shape[1], done.shape[3]
    wide = width + LANES
    chunks = width // LANES
    levels = SUB // 2

    def copies_out(source, source_row, row, count):
        copies = []
        for level in range(levels):
            for half in range(2):
                s = 2 * level + half
                rows, to = pl.ds(source_row, count), pl.ds(half * half_rows + row, count)
                copies += [
                    pltpu.make_async_copy(source.at[0:2, rows, s, :], vel_out.at[:, level, to, :], sem),
                    pltpu.make_async_copy(source.at[2, rows, s, :], thick_out.at[level, to, :], sem),
                    pltpu.make_async_copy(source.at[3:5, rows, s, :], trac_out.at[:, level, to, :], sem),
                ]
        for copy in copies:
            copy.start()
        return copies

    copies = copies_out(done, PAD, PAD, half_rows - 2 * PAD)
    for f in range(5):
        for i in range(HALO):
            strip[f, HALO + i] = done[f, HALO + i]
            strip[f, PAD + i] = done[f, half_rows - PAD + i]
    lat = lax.axis_index("lat")
    lat_even, southmost = lat % 2 == 0, lat == 0
    even, even_one = even_half(wide), even_half(LANES)
    even_out = even_half(width)
    corner_a, corner_b = rows_a[chunks * SLOTS], rows_b[chunks * SLOTS]

    def message(ref, corner, slot):
        parts = [ref[chunks * slot + c] for c in range(chunks)]
        return jnp.concatenate([*parts, pltpu.roll(corner, -(8 * slot + HALO) % LANES, 1)], axis=1)

    for f in range(6):
        reach = HALO if f < 5 else 2
        for m in range(reach // 2):
            slot, opposite = 2 * f + m, 2 * f + reach // 2 - 1 - m
            south = [message(ref, corner, slot) for ref, corner in ((rows_a, corner_a), (rows_b, corner_b))]
            north = [message(ref, corner, opposite) for ref, corner in ((rows_a, corner_a), (rows_b, corner_b))]
            from_south = jnp.where(southmost, 0.0, jnp.where(lat_even, south[1], south[0]))
            from_north = jnp.where(lat_even, north[0], north[1])
            row = 2 * m - reach
            first[f, row + HALO] = jnp.where(even, pltpu.roll(from_south, SUB - 1, 0), from_north)
            first[f, row + 1 + HALO] = jnp.where(even, from_south, pltpu.roll(from_north, 1, 0))

    def whole(f, i):
        return first[f, i + HALO] if i < 0 else joint[f, i]

    def halfway(f, i):
        return second[f, i + 2] if i < 2 else ring[f, i - 2]

    def keep(f, i, value):
        second[f, i + 2] = value

    def write(f, i, value):
        other = middle[f, i]
        strip[f, i] = jnp.where(even_out, value, other)
        strip[f, 2 * PAD - 1 - i] = jnp.where(even_out, other, value)

    ahead_row, update_row = make_step(wide, sums, east_diff, press)
    north_even = jnp.where(even, 1.0, -1.0)

    def sweep(source, step, low, cut, emit):
        high = low + 4
        for k in range(2):
            for f in range(5):
                sums[f, high - 1 + k + 4] = joint_sums[step, f, k]
            press[high - 1 + k + 4] = joint_press[step, k]
        for f in range(5):
            east_diff[f, high - 1 + 4] = joint_diff[step, f]
        ahead_row(source, low - 1, low + 3)
        ahead_row(source, low, low + 4)
        for i in range(low, high):
            if i + 1 < high - 1:
                ahead_row(source, i + 1, i + 5)
            turn = jnp.where(even_one, coriolis[i + PAD], coriolis[half_rows - 1 - i + PAD])
            update_row(source, whole(5, i)[:, :cut], turn, i, i + 4, cut, emit, north_even)

    sweep(whole, 0, -2, wide, keep)
    sweep(halfway, 1, 0, width, write)
    copies += copies_out(strip, 0, 0, PAD)
    copies += copies_out(strip, PAD, half_rows - PAD, PAD)
    for copy in copies:
        copy.wait()


def lat_pairs(parity, lat_count, lon_count):
    pairs = []
    for lat in range(lat_count):
        for lon in range(lon_count):
            to_lat, to_lon = (lat + 1 if lat % 2 == parity else lat - 1), lon
            if to_lat < 0:
                to_lat, to_lon = 0, lon ^ 1
            if to_lat == lat_count:
                to_lat, to_lon = lat, lon_count - 1 - lon
            pairs.append((lon * lat_count + lat, to_lon * lat_count + to_lat))
    return pairs


def lon_pairs(parity, lon_count):
    return [(i, (i + 1 if i % 2 == parity else i - 1) % lon_count) for i in range(lon_count)]


def shapes(*dims):
    return jax.ShapeDtypeStruct(dims, F32)


def body(lat_count, lon_count, velocity, thickness, tracers, land_mask):
    levels, rows, width = thickness.shape
    half_rows = rows // 2
    wide, tall = width + LANES, half_rows + 2 * PAD
    arguments = (velocity, thickness, tracers, land_mask)
    fields = [pltpu.with_memory_space_constraint(x, pltpu.HBM) for x in arguments]
    dma = pltpu.SemaphoreType.DMA

    def call(kernel, name, in_specs, outs, out_specs, scratch, flops):
        return pl.pallas_call(
            kernel,
            out_shape=outs,
            in_specs=in_specs,
            out_specs=out_specs,
            scratch_shapes=scratch,
            compiler_params=pltpu.CompilerParams(vmem_limit_bytes=24 * 2**20),
            cost_estimate=pl.CostEstimate(flops=flops, bytes_accessed=flops // 10, transcendentals=0),
            name=name,
        )

    columns = shapes(6, SUB, LANES)
    send_a, send_b = call(
        columns_kernel,
        "pack_columns",
        [HBM] * 4,
        (columns, columns),
        (VMEM, VMEM),
        [pltpu.VMEM((5, half_rows, SUB, 2 * LANES), F32), pltpu.VMEM((half_rows, SUB, 2 * LANES), jnp.int32), dma((6,))],
        10**6,
    )(*fields)
    cols_a = lax.ppermute(send_a, "lon", lon_pairs(0, lon_count))
    cols_b = lax.ppermute(send_b, "lon", lon_pairs(1, lon_count))

    block = shapes(ROLLED, tall, SUB, width)
    planes, from_east, from_west, coriolis = call(
        functools.partial(load_kernel, lat_count),
        "load_fields",
        [HBM, HBM, HBM, HBM, ANY],
        (shapes(6, tall, SUB, width), block, block, shapes(tall, SUB, LANES)),
        (VMEM,) * 4,
        [pltpu.VMEM((tall, SUB, width), jnp.int32), dma((6,))],
        10**8,
    )(*fields, send_a)

    message = shapes(SLOTS * (width // LANES) + 1, SUB, LANES)
    send_a, send_b = call(
        functools.partial(rows_kernel, lat_count),
        "pack_rows",
        [VMEM] * 3,
        (message, message),
        (VMEM, VMEM),
        [],
        10**6,
    )(planes, cols_a, cols_b)
    axes = ("lon", "lat")
    rows_a = lax.ppermute(send_a, axes, lat_pairs(0, lat_count, lon_count))
    rows_b = lax.ppermute(send_b, axes, lat_pairs(1, lat_count, lon_count))

    def work(length):
        tall_planes = pltpu.VMEM((5, length, SUB, wide), F32)
        return [tall_planes, tall_planes, pltpu.VMEM((length, SUB, wide), F32)]

    done, middle, *kept = call(
        interior_kernel,
        "interior",
        [VMEM] * 6 + [ANY],
        (
            shapes(5, half_rows, SUB, width),
            shapes(5, 4, SUB, width),
            shapes(6, 4, SUB, wide),
            shapes(5, 4, SUB, wide),
            shapes(2, 5, 2, SUB, wide),
            shapes(2, 5, SUB, wide),
            shapes(2, 2, SUB, wide),
        ),
        (VMEM,) * 7,
        [
            pltpu.VMEM((6, tall, SUB, LANES), F32),
            pltpu.VMEM((2, 6, SUB, LANES), F32),
            pltpu.VMEM((5, tall, SUB, wide), F32),
            pltpu.VMEM((5, 4, SUB, wide), F32),
            *work(tall),
        ],
        10**8,
    )(planes, from_east, from_west, cols_a, cols_b, coriolis, send_a)

    return call(
        edges_kernel,
        "edges",
        [VMEM] * 10,
        (shapes(*velocity.shape), shapes(*thickness.shape), shapes(*tracers.shape)),
        (HBM, HBM, HBM),
        [
            pltpu.VMEM((5, 2 * PAD, SUB, width), F32),
            pltpu.VMEM((6, HALO, SUB, wide), F32),
            pltpu.VMEM((5, 4, SUB, wide), F32),
            *work(10),
            dma,
        ],
        10**8,
    )(*kept, middle, coriolis, done, rows_a, rows_b)


def solution(mesh):
    specs = (P(None, None, "lat", "lon"), P(None, "lat", "lon"), P(None, None, "lat", "lon"))
    return jax.shard_map(
        functools.partial(body, mesh.shape["lat"], mesh.shape["lon"]),
        mesh=mesh,
        in_specs=(*specs, P(None, "lat", "lon")),
        out_specs=specs,
        check_vma=False,
    )
```

```python
import functools

import jax
import jax.numpy as jnp
from jax import lax
from jax.experimental import pallas as pl
from jax.experimental.pallas import tpu as pltpu
from jax.sharding import PartitionSpec as P

ADVECTION = 0.25
DIFFUSION = 0.05
HYPERVISCOSITY = 0.02
CORIOLIS = 0.3
GRADIENT = 0.2
CONVERGENCE = 0.3

HALO = 4
PAD = 8
LANES = 128
SUB = 8
SLOTS = 11
ROLLED = 4
F32 = jnp.float32
VMEM = pl.BlockSpec(memory_space=pltpu.VMEM)
HBM = pl.BlockSpec(memory_space=pltpu.HBM)
ANY = pl.BlockSpec(memory_space=pl.ANY)


def even_half(lanes):
    return lax.broadcasted_iota(jnp.int32, (SUB, lanes), 0) % 2 == 0


def flip_lanes(values):
    index = LANES - 1 - lax.broadcasted_iota(jnp.int32, (SUB, LANES), 1)
    chunks = range(0, values.shape[-1], LANES)
    parts = [jnp.take_along_axis(values[:, c : c + LANES], index, axis=1) for c in reversed(chunks)]
    return jnp.concatenate(parts, axis=1)


def columns_kernel(vel, thick, trac, mask, out_a, out_b, edges, land, sem):
    levels, rows, width = thick.shape
    half_rows = rows // 2
    groups = {0: [], 2: [], 3: [], 5: []}
    for side in range(2):
        lanes = pl.ds(side * (width - LANES), LANES)
        to = pl.ds(side * LANES, LANES)
        for level in range(levels):
            for half in range(2):
                at, s = pl.ds(half * half_rows, half_rows), 2 * level + half
                for f, source, target in (
                    (0, vel.at[:, level, at, lanes], edges.at[0:2, :, s, to]),
                    (2, thick.at[level, at, lanes], edges.at[2, :, s, to]),
                    (3, trac.at[:, level, at, lanes], edges.at[3:5, :, s, to]),
                    (5, mask.at[level, at, lanes], land.at[:, s, to]),
                ):
                    groups[f].append(pltpu.make_async_copy(source, target, sem.at[f]))
    for f in groups:
        for copy in groups[f]:
            copy.start()
    lon_even = lax.axis_index("lon") % 2 == 0
    group = lax.broadcasted_iota(jnp.int32, (SUB, LANES), 1) // HALO
    for f in range(6):
        for copy in groups.get(f, ()):
            copy.wait()
        west = east = jnp.zeros((SUB, LANES), F32)
        for row in range(half_rows):
            pair = edges[f, row] if f < 5 else HYPERVISCOSITY * land[row].astype(F32)
            here = group == row
            west = jnp.where(here, pltpu.roll(pair[:, :LANES], HALO * row % LANES, 1), west)
            east = jnp.where(here, pltpu.roll(pair[:, LANES:], HALO * (row + 1) % LANES, 1), east)
        out_a[f] = jnp.where(lon_even, east, west)
        out_b[f] = jnp.where(lon_even, west, east)


def load_kernel(lat_count, vel, thick, trac, mask, after, planes, from_east, from_west, coriolis, land, sem):
    del after
    levels, rows, width = thick.shape
    half_rows = rows // 2
    length = half_rows + PAD
    groups = {0: [], 2: [], 3: [], 5: []}
    for level in range(levels):
        for half in range(2):
            at, s = pl.ds(half * (half_rows - PAD), length), 2 * level + half
            to = pl.ds((1 - half) * PAD, length)
            for f, source, target in (
                (0, vel.at[:, level, at, :], planes.at[0:2, to, s, :]),
                (2, thick.at[level, at, :], planes.at[2, to, s, :]),
                (3, trac.at[:, level, at, :], planes.at[3:5, to, s, :]),
                (5, mask.at[level, at, :], land.at[to, s, :]),
            ):
                groups[f].append(pltpu.make_async_copy(source, target, sem.at[f]))
    for f in groups:
        for copy in groups[f]:
            copy.start()
    total = rows * lat_count
    half = lax.broadcasted_iota(jnp.int32, (SUB, LANES), 0) % 2
    first = lax.axis_index("lat") * rows + half * half_rows
    for row in range(-2, half_rows + 2):
        ids = first + row
        folded = jnp.where(ids >= total, 2 * total - 1 - ids, ids)
        angle = jnp.pi * (folded.astype(F32) + 0.5) / total - jnp.pi / 2
        coriolis[row + PAD] = (CORIOLIS / HYPERVISCOSITY) * jnp.sin(angle)
    for f in range(6):
        for copy in groups.get(f, ()):
            copy.wait()
        if f == 5:
            break
        for row in range(PAD, half_rows + PAD) if f < ROLLED else ():
            value = planes[f, row]
            from_east[f, row] = pltpu.roll(value, width - 1, 1)
            from_west[f, row] = pltpu.roll(value, 1, 1)
    for row in range(PAD - 2, half_rows + PAD + 2):
        planes[5, row] = HYPERVISCOSITY * land[row].astype(F32)


def halo_columns(cols_a, cols_b, lon_even):
    def get(f):
        a, b = cols_a[f], cols_b[f]
        return halo_of(jnp.where(lon_even, a, b), jnp.where(lon_even, b, a))

    return get


def halo_of(from_east, from_west):
    lane = lax.broadcasted_iota(jnp.int32, (SUB, LANES), 1)

    def row(r):
        east = pltpu.roll(from_east, (LANES - HALO * r) % LANES, 1)
        west = pltpu.roll(from_west, LANES - HALO * (r + 1), 1)
        return jnp.where(lane < LANES // 2, east, west)

    return row


def rows_kernel(lat_count, planes, cols_a, cols_b, out_a, out_b):
    half_rows, width = planes.shape[1] - 2 * PAD, planes.shape[3]
    chunks = width // LANES
    lat = lax.axis_index("lat")
    lat_even = lat % 2 == 0
    lon_even = lax.axis_index("lon") % 2 == 0
    even = even_half(width + LANES)
    group = lax.broadcasted_iota(jnp.int32, (SUB, LANES), 1) // 8
    get = halo_columns(cols_a, cols_b, lon_even)
    column = [get(f) for f in range(6)]
    slots = [(f, m) for f in range(5) for m in range(2)] + [(5, None)]

    def whole(f, row):
        return jnp.concatenate([planes[f, row + PAD], column[f](row)], axis=1)

    def north(f, m):
        low = half_rows - HALO + 2 * m
        return jnp.where(even, pltpu.roll(whole(f, low + 1), SUB - 1, 0), whole(f, low))

    def south(f, m):
        return jnp.where(even, whole(f, 2 * m), pltpu.roll(whole(f, 2 * m + 1), 1, 0))

    def put(target, slot, value):
        for c in range(chunks):
            target[chunks * slot + c] = value[:, c * LANES : (c + 1) * LANES]

    def add_corner(corner, slot, value):
        return jnp.where(group == slot, pltpu.roll(value[:, width:], 8 * slot + HALO, 1), corner)

    corner_a = corner_b = jnp.zeros((SUB, LANES), F32)
    for slot, (f, m) in enumerate(slots):
        to_north = north(f, 1 if m is None else m)
        to_south = south(f, 0 if m is None else m)
        a = jnp.where(lat_even, to_north, to_south)
        b = jnp.where(lat_even, to_south, to_north)
        put(out_a, slot, a)
        put(out_b, slot, b)
        corner_a = add_corner(corner_a, slot, a)
        corner_b = add_corner(corner_b, slot, b)
    out_a[chunks * SLOTS] = corner_a
    out_b[chunks * SLOTS] = corner_b

    @pl.when(lat == lat_count - 1)
    def _():
        target = out_a if (lat_count - 1) % 2 == 0 else out_b
        corner = jnp.zeros((SUB, LANES), F32)
        for slot, (f, m) in enumerate(slots):
            value = north(f, 1 if m is None else 1 - m)
            value = -value if f < 2 else value
            mirrored = jnp.concatenate([flip_lanes(value[:, :width]), flip_lanes(value[:, width:])], axis=1)
            put(target, slot, mirrored)
            corner = add_corner(corner, slot, mirrored)
        target[chunks * SLOTS] = corner


def make_step(wide, sums, east_diff, press):
    scale = 1.0 / HYPERVISCOSITY
    keep_own = scale * (1.0 - 4.0 * DIFFUSION - 16.0 * HYPERVISCOSITY)
    keep_sum = scale * (DIFFUSION + 8.0 * HYPERVISCOSITY)
    advect = -0.5 * ADVECTION * scale
    slope = -0.5 * GRADIENT * scale
    converge = -0.5 * CONVERGENCE * scale
    level = lax.broadcasted_iota(jnp.int32, (SUB, wide), 0) // 2
    weight = slope / (level.astype(F32) + 1.0)
    below_one, below_two = level >= 1, level >= 2

    def shifts(value):
        return pltpu.roll(value, wide - 1, 1), pltpu.roll(value, 1, 1)

    def ahead(source, row, at, f, shifted, cut):
        to_east, to_west = shifted(f, row) if shifted else shifts(source(f, row))
        sums[f, at] = (to_east + to_west) + (source(f, row + 1) + source(f, row - 1))
        east_diff[f, at, :, :cut] = (to_east - to_west)[:, :cut]

    def weighed_down(thick, temp, salt):
        lanes = slice(0, thick.shape[-1])
        part = weight[:, lanes] * thick + ((0.08 * slope) * salt - (0.1 * slope) * temp)
        part = part + jnp.where(below_one[:, lanes], pltpu.roll(part, 2, 0), 0.0)
        return part + jnp.where(below_two[:, lanes], pltpu.roll(part, 4, 0), 0.0)

    def ahead_press(source, row, at, cut):
        press[at, :, :cut] = weighed_down(*(source(f, row)[:, :cut] for f in (2, 3, 4)))

    def update_row(source, ocean, turn, row, at, cut, emit, northward=None, roll_press=False):
        lanes = slice(0, cut)
        turn = jnp.concatenate([turn] * (cut // LANES), axis=1)
        u, v = source(0, row)[:, lanes], source(1, row)[:, lanes]
        along_u, along_v = advect * u, advect * v
        if northward is not None:
            along_v = along_v * northward[:, lanes]

        def add_on(f):
            if f == 0:
                if roll_press:
                    p_east, p_west = shifts(press[at])
                    return turn * v + (p_east - p_west)[:, lanes]
                slopes = [east_diff[field, at, :, lanes] for field in (2, 3, 4)]
                return turn * v + weighed_down(*slopes)
            if f == 1:
                rise = press[at + 1, :, lanes] - press[at - 1, :, lanes]
                if northward is not None:
                    rise = rise * northward[:, lanes]
                return rise - turn * u
            v_north = source(1, row + 1)[:, lanes] - source(1, row - 1)[:, lanes]
            if northward is not None:
                v_north = v_north * northward[:, lanes]
            return converge * (east_diff[0, at, :, lanes] + v_north)

        def one(f):
            here = sums[f, at]
            s_east, s_west = shifts(here)
            around = (s_east + s_west)[:, lanes] + (sums[f, at + 1, :, lanes] + sums[f, at - 1, :, lanes])
            dx = east_diff[f, at, :, lanes]
            dy = source(f, row + 1)[:, lanes] - source(f, row - 1)[:, lanes]
            value = keep_own * source(f, row)[:, lanes] + (keep_sum * here[:, lanes] - around)
            value = value + (along_u * dx + along_v * dy)
            if f < 3:
                value = value + add_on(f)
            emit(f, row, value * ocean)

        for f in range(5):
            one(f)

    def ahead_row(source, row, at, cut, shifted=None):
        ahead_press(source, row, at, cut)
        for f in range(5):
            ahead(source, row, at, f, shifted, cut)

    return ahead_row, update_row


def swap_halves(value):
    even = even_half(value.shape[-1])
    return jnp.where(even, pltpu.roll(value, SUB - 1, 0), pltpu.roll(value, 1, 0))


def interior_kernel(
    planes,
    from_east,
    from_west,
    cols_a,
    cols_b,
    coriolis,
    after,
    out,
    middle,
    joint,
    ring,
    joint_sums,
    joint_diff,
    joint_press,
    outer,
    sides,
    second,
    centre,
    sums,
    east_diff,
    press,
):
    del after
    half_rows, width = planes.shape[1] - 2 * PAD, planes.shape[3]
    last = half_rows - 1
    wide = width + LANES
    lon_even = lax.axis_index("lon") % 2 == 0
    for f in range(6):
        a, b = cols_a[f], cols_b[f]
        sides[0, f] = jnp.where(lon_even, a, b)
        sides[1, f] = jnp.where(lon_even, b, a)

    def add_halo(row):
        for f in range(6):
            outer[f, row + PAD] = halo_of(sides[0, f], sides[1, f])(row)

    for row in range(4):
        add_halo(row)
    ahead_row, update_row = make_step(wide, sums, east_diff, press)
    even = even_half(wide)
    lane = lax.broadcasted_iota(jnp.int32, (SUB, LANES), 1)
    at_first, at_last = lane == 0, lane == LANES - 1

    def whole(f, row):
        return jnp.concatenate([planes[f, row + PAD], outer[f, row + PAD]], axis=1)

    def whole_shifted(f, row):
        at = row + PAD
        if f >= ROLLED:
            return pltpu.roll(whole(f, row), wide - 1, 1), pltpu.roll(whole(f, row), 1, 1)
        east, west, halo = from_east[f, at], from_west[f, at], outer[f, at]
        halo_east, halo_west = pltpu.roll(halo, LANES - 1, 1), pltpu.roll(halo, 1, 1)
        tail, head = east[:, width - LANES :], west[:, :LANES]
        east = [east[:, : width - LANES], jnp.where(at_last, halo_east, tail), jnp.where(at_last, tail, halo_east)]
        west = [jnp.where(at_first, halo_west, head), west[:, LANES:], jnp.where(at_first, head, halo_west)]
        return jnp.concatenate(east, axis=1), jnp.concatenate(west, axis=1)

    def keep(f, row, value):
        second[f, row + PAD] = value

    def halfway(f, row):
        return second[f, row + PAD]

    def write(f, row, value):
        out[f, row] = value

    def sweep(source, low, high, cut, emit, shifted=None):
        ahead_row(source, low - 1, low - 1 + PAD, cut, shifted)
        ahead_row(source, low, low + PAD, cut, shifted)

        def iteration(row, carry):
            if shifted:
                add_halo(row + 2)
            ahead_row(source, row + 1, row + 1 + PAD, cut, shifted)
            ocean, turn = whole(5, row)[:, :cut], coriolis[row + PAD]
            update_row(source, ocean, turn, row, row + PAD, cut, emit, roll_press=bool(shifted))
            return carry

        lax.fori_loop(low, high, iteration, 0, unroll=(high - low) // 2)

    def outer_pair(ref, i):
        return jnp.where(even, ref[i + PAD], ref[last - i + PAD])

    def inner_pair(ref, i):
        return jnp.where(even, ref[last - i + PAD], ref[i + PAD])

    def save_outer(step, i):
        for f in range(5):
            for k in range(2):
                joint_sums[step, f, k] = outer_pair(sums.at[f], i + k)
            joint_diff[step, f] = outer_pair(east_diff.at[f], i)
        for k in range(2):
            joint_press[step, k] = outer_pair(press, i + k)

    def take_inner(i):
        for f in range(5):
            sums[f, i + 1] = inner_pair(sums.at[f], i)
            east_diff[f, i + 1] = inner_pair(east_diff.at[f], i)
        press[i + 1] = inner_pair(press, i)

    def fold_inner():
        for f in range(5):
            sums[f, 0] = swap_halves(sums[f, 1])
        press[0] = swap_halves(press[1])

    sweep(whole, 2, half_rows - 2, wide, keep, whole_shifted)
    for f in range(5):
        outer[f, half_rows + PAD] = pltpu.roll(outer[f, PAD], SUB - 1, 0)
        outer[f, PAD - 1] = pltpu.roll(outer[f, last + PAD], 1, 0)
    save_outer(0, 1)
    for i in range(4):
        for f in range(6):
            joint[f, i] = jnp.where(even, whole(f, i), whole(f, last - i))
        for f in range(5):
            ring[f, i] = outer_pair(second.at[f], 2 + i)

    def mirrored(f, i):
        return jnp.where(even, whole(f, last - i), whole(f, i))

    def mirrored_shifted(f, i):
        south, north = whole_shifted(f, last - i), whole_shifted(f, i)
        return [jnp.where(even, one, other) for one, other in zip(south, north)]

    north_odd = jnp.where(even, -1.0, 1.0)

    def turn_of(i):
        return jnp.where(even[:, :LANES], coriolis[last - i + PAD], coriolis[i + PAD])

    def keep_centre(f, i, value):
        centre[f, i + 2] = value
        centre[f, 1 - i] = swap_halves(value)

    ahead_row(mirrored, 0, 1, wide, mirrored_shifted)
    fold_inner()
    take_inner(1)
    take_inner(2)
    for i in range(2):
        update_row(mirrored, mirrored(5, i), turn_of(i), i, i + 1, wide, keep_centre, north_odd)

    sweep(halfway, HALO, half_rows - HALO, width, write)
    save_outer(1, 3)

    def centre_halfway(f, i):
        return centre[f, i + 2] if i < 2 else inner_pair(second.at[f], i)

    def keep_middle(f, i, value):
        middle[f, i] = value

    for i in range(3):
        ahead_row(centre_halfway, i, i + 1, width)
    fold_inner()
    take_inner(3)
    take_inner(4)
    for i in range(4):
        ocean = mirrored(5, i)[:, :width]
        update_row(centre_halfway, ocean, turn_of(i), i, i + 1, width, keep_middle, north_odd)


def edges_kernel(
    joint,
    ring,
    joint_sums,
    joint_diff,
    joint_press,
    middle,
    coriolis,
    done,
    rows_a,
    rows_b,
    vel_out,
    thick_out,
    trac_out,
    strip,
    first,
    second,
    sums,
    east_diff,
    press,
    sem,
):
    half_rows, width = done.shape[1], done.shape[3]
    wide = width + LANES
    chunks = width // LANES
    levels = SUB // 2

    def copies_out(source, source_row, row, count):
        copies = []
        for level in range(levels):
            for half in range(2):
                s = 2 * level + half
                rows, to = pl.ds(source_row, count), pl.ds(half * half_rows + row, count)
                copies += [
                    pltpu.make_async_copy(source.at[0:2, rows, s, :], vel_out.at[:, level, to, :], sem),
                    pltpu.make_async_copy(source.at[2, rows, s, :], thick_out.at[level, to, :], sem),
                    pltpu.make_async_copy(source.at[3:5, rows, s, :], trac_out.at[:, level, to, :], sem),
                ]
        for copy in copies:
            copy.start()
        return copies

    copies = copies_out(done, PAD, PAD, half_rows - 2 * PAD)
    for f in range(5):
        for i in range(HALO):
            strip[f, HALO + i] = done[f, HALO + i]
            strip[f, PAD + i] = done[f, half_rows - PAD + i]
    lat = lax.axis_index("lat")
    lat_even, southmost = lat % 2 == 0, lat == 0
    even, even_one = even_half(wide), even_half(LANES)
    even_out = even_half(width)
    corner_a, corner_b = rows_a[chunks * SLOTS], rows_b[chunks * SLOTS]

    def message(ref, corner, slot):
        parts = [ref[chunks * slot + c] for c in range(chunks)]
        return jnp.concatenate([*parts, pltpu.roll(corner, -(8 * slot + HALO) % LANES, 1)], axis=1)

    for f in range(6):
        reach = HALO if f < 5 else 2
        for m in range(reach // 2):
            slot, opposite = 2 * f + m, 2 * f + reach // 2 - 1 - m
            south = [message(ref, corner, slot) for ref, corner in ((rows_a, corner_a), (rows_b, corner_b))]
            north = [message(ref, corner, opposite) for ref, corner in ((rows_a, corner_a), (rows_b, corner_b))]
            from_south = jnp.where(southmost, 0.0, jnp.where(lat_even, south[1], south[0]))
            from_north = jnp.where(lat_even, north[0], north[1])
            row = 2 * m - reach
            first[f, row + HALO] = jnp.where(even, pltpu.roll(from_south, SUB - 1, 0), from_north)
            first[f, row + 1 + HALO] = jnp.where(even, from_south, pltpu.roll(from_north, 1, 0))

    def whole(f, i):
        return first[f, i + HALO] if i < 0 else joint[f, i]

    def halfway(f, i):
        return second[f, i + 2] if i < 2 else ring[f, i - 2]

    def keep(f, i, value):
        second[f, i + 2] = value

    def write(f, i, value):
        other = middle[f, i]
        strip[f, i] = jnp.where(even_out, value, other)
        strip[f, 2 * PAD - 1 - i] = jnp.where(even_out, other, value)

    ahead_row, update_row = make_step(wide, sums, east_diff, press)
    north_even = jnp.where(even, 1.0, -1.0)

    def sweep(source, step, low, cut, emit):
        high = low + 4
        for k in range(2):
            for f in range(5):
                sums[f, high - 1 + k + 4] = joint_sums[step, f, k]
            press[high - 1 + k + 4] = joint_press[step, k]
        for f in range(5):
            east_diff[f, high - 1 + 4] = joint_diff[step, f]
        ahead_row(source, low - 1, low + 3, cut)
        ahead_row(source, low, low + 4, cut)
        for i in range(low, high):
            if i + 1 < high - 1:
                ahead_row(source, i + 1, i + 5, cut)
            turn = jnp.where(even_one, coriolis[i + PAD], coriolis[half_rows - 1 - i + PAD])
            update_row(source, whole(5, i)[:, :cut], turn, i, i + 4, cut, emit, north_even)

    sweep(whole, 0, -2, wide, keep)
    sweep(halfway, 1, 0, width, write)
    copies += copies_out(strip, 0, 0, PAD)
    copies += copies_out(strip, PAD, half_rows - PAD, PAD)
    for copy in copies:
        copy.wait()


def lat_pairs(parity, lat_count, lon_count):
    pairs = []
    for lat in range(lat_count):
        for lon in range(lon_count):
            to_lat, to_lon = (lat + 1 if lat % 2 == parity else lat - 1), lon
            if to_lat < 0:
                to_lat, to_lon = 0, lon ^ 1
            if to_lat == lat_count:
                to_lat, to_lon = lat, lon_count - 1 - lon
            pairs.append((lon * lat_count + lat, to_lon * lat_count + to_lat))
    return pairs


def lon_pairs(parity, lon_count):
    return [(i, (i + 1 if i % 2 == parity else i - 1) % lon_count) for i in range(lon_count)]


def shapes(*dims):
    return jax.ShapeDtypeStruct(dims, F32)


def body(lat_count, lon_count, velocity, thickness, tracers, land_mask):
    levels, rows, width = thickness.shape
    half_rows = rows // 2
    wide, tall = width + LANES, half_rows + 2 * PAD
    arguments = (velocity, thickness, tracers, land_mask)
    fields = [pltpu.with_memory_space_constraint(x, pltpu.HBM) for x in arguments]
    dma = pltpu.SemaphoreType.DMA

    def call(kernel, name, in_specs, outs, out_specs, scratch, flops):
        return pl.pallas_call(
            kernel,
            out_shape=outs,
            in_specs=in_specs,
            out_specs=out_specs,
            scratch_shapes=scratch,
            compiler_params=pltpu.CompilerParams(vmem_limit_bytes=24 * 2**20),
            cost_estimate=pl.CostEstimate(flops=flops, bytes_accessed=flops // 10, transcendentals=0),
            name=name,
        )

    columns = shapes(6, SUB, LANES)
    send_a, send_b = call(
        columns_kernel,
        "pack_columns",
        [HBM] * 4,
        (columns, columns),
        (VMEM, VMEM),
        [pltpu.VMEM((5, half_rows, SUB, 2 * LANES), F32), pltpu.VMEM((half_rows, SUB, 2 * LANES), jnp.int32), dma((6,))],
        10**6,
    )(*fields)
    cols_a = lax.ppermute(send_a, "lon", lon_pairs(0, lon_count))
    cols_b = lax.ppermute(send_b, "lon", lon_pairs(1, lon_count))

    block = shapes(ROLLED, tall, SUB, width)
    planes, from_east, from_west, coriolis = call(
        functools.partial(load_kernel, lat_count),
        "load_fields",
        [HBM, HBM, HBM, HBM, ANY],
        (shapes(6, tall, SUB, width), block, block, shapes(tall, SUB, LANES)),
        (VMEM,) * 4,
        [pltpu.VMEM((tall, SUB, width), jnp.int32), dma((6,))],
        10**8,
    )(*fields, send_a)

    message = shapes(SLOTS * (width // LANES) + 1, SUB, LANES)
    send_a, send_b = call(
        functools.partial(rows_kernel, lat_count),
        "pack_rows",
        [VMEM] * 3,
        (message, message),
        (VMEM, VMEM),
        [],
        10**6,
    )(planes, cols_a, cols_b)
    axes = ("lon", "lat")
    rows_a = lax.ppermute(send_a, axes, lat_pairs(0, lat_count, lon_count))
    rows_b = lax.ppermute(send_b, axes, lat_pairs(1, lat_count, lon_count))

    def work(length):
        tall_planes = pltpu.VMEM((5, length, SUB, wide), F32)
        return [tall_planes, tall_planes, pltpu.VMEM((length, SUB, wide), F32)]

    done, middle, *kept = call(
        interior_kernel,
        "interior",
        [VMEM] * 6 + [ANY],
        (
            shapes(5, half_rows, SUB, width),
            shapes(5, 4, SUB, width),
            shapes(6, 4, SUB, wide),
            shapes(5, 4, SUB, wide),
            shapes(2, 5, 2, SUB, wide),
            shapes(2, 5, SUB, wide),
            shapes(2, 2, SUB, wide),
        ),
        (VMEM,) * 7,
        [
            pltpu.VMEM((6, tall, SUB, LANES), F32),
            pltpu.VMEM((2, 6, SUB, LANES), F32),
            pltpu.VMEM((5, tall, SUB, wide), F32),
            pltpu.VMEM((5, 4, SUB, wide), F32),
            *work(tall),
        ],
        10**8,
    )(planes, from_east, from_west, cols_a, cols_b, coriolis, send_b)

    return call(
        edges_kernel,
        "edges",
        [VMEM] * 10,
        (shapes(*velocity.shape), shapes(*thickness.shape), shapes(*tracers.shape)),
        (HBM, HBM, HBM),
        [
            pltpu.VMEM((5, 2 * PAD, SUB, width), F32),
            pltpu.VMEM((6, HALO, SUB, wide), F32),
            pltpu.VMEM((5, 4, SUB, wide), F32),
            *work(10),
            dma,
        ],
        10**8,
    )(*kept, middle, coriolis, done, rows_a, rows_b)


def solution(mesh):
    specs = (P(None, None, "lat", "lon"), P(None, "lat", "lon"), P(None, None, "lat", "lon"))
    return jax.shard_map(
        functools.partial(body, mesh.shape["lat"], mesh.shape["lon"]),
        mesh=mesh,
        in_specs=(*specs, P(None, "lat", "lon")),
        out_specs=specs,
        check_vma=False,
    )
```

```python
import functools

import jax
import jax.numpy as jnp
from jax import lax
from jax.experimental import pallas as pl
from jax.experimental.pallas import tpu as pltpu
from jax.sharding import PartitionSpec as P

ADVECTION = 0.25
DIFFUSION = 0.05
HYPERVISCOSITY = 0.02
CORIOLIS = 0.3
GRADIENT = 0.2
CONVERGENCE = 0.3

HALO = 4
PAD = 8
LANES = 128
SUB = 8
SLOTS = 11
ROLLED = 4
F32 = jnp.float32
VMEM = pl.BlockSpec(memory_space=pltpu.VMEM)
HBM = pl.BlockSpec(memory_space=pltpu.HBM)
ANY = pl.BlockSpec(memory_space=pl.ANY)


def even_half(lanes):
    return lax.broadcasted_iota(jnp.int32, (SUB, lanes), 0) % 2 == 0


def flip_lanes(values):
    index = LANES - 1 - lax.broadcasted_iota(jnp.int32, (SUB, LANES), 1)
    chunks = range(0, values.shape[-1], LANES)
    parts = [jnp.take_along_axis(values[:, c : c + LANES], index, axis=1) for c in reversed(chunks)]
    return jnp.concatenate(parts, axis=1)


def columns_kernel(vel, thick, trac, mask, out_a, out_b, edges, land, sem):
    levels, rows, width = thick.shape
    half_rows = rows // 2
    groups = {0: [], 2: [], 3: [], 5: []}
    for side in range(2):
        lanes = pl.ds(side * (width - LANES), LANES)
        to = pl.ds(side * LANES, LANES)
        for level in range(levels):
            for half in range(2):
                at, s = pl.ds(half * half_rows, half_rows), 2 * level + half
                for f, source, target in (
                    (0, vel.at[:, level, at, lanes], edges.at[0:2, :, s, to]),
                    (2, thick.at[level, at, lanes], edges.at[2, :, s, to]),
                    (3, trac.at[:, level, at, lanes], edges.at[3:5, :, s, to]),
                    (5, mask.at[level, at, lanes], land.at[:, s, to]),
                ):
                    groups[f].append(pltpu.make_async_copy(source, target, sem.at[f]))
    for f in groups:
        for copy in groups[f]:
            copy.start()
    lon_even = lax.axis_index("lon") % 2 == 0
    group = lax.broadcasted_iota(jnp.int32, (SUB, LANES), 1) // HALO
    for f in range(6):
        for copy in groups.get(f, ()):
            copy.wait()
        west = east = jnp.zeros((SUB, LANES), F32)
        for row in range(half_rows):
            pair = edges[f, row] if f < 5 else HYPERVISCOSITY * land[row].astype(F32)
            here = group == row
            west = jnp.where(here, pltpu.roll(pair[:, :LANES], HALO * row % LANES, 1), west)
            east = jnp.where(here, pltpu.roll(pair[:, LANES:], HALO * (row + 1) % LANES, 1), east)
        out_a[f] = jnp.where(lon_even, east, west)
        out_b[f] = jnp.where(lon_even, west, east)


def load_kernel(lat_count, vel, thick, trac, mask, after, planes, from_east, from_west, coriolis, land, sem):
    del after
    levels, rows, width = thick.shape
    half_rows = rows // 2
    groups = {0: [], 2: [], 3: [], 5: []}
    for level in range(levels):
        for half in range(2):
            at, s = pl.ds(half * half_rows, half_rows), 2 * level + half
            to = pl.ds(PAD, half_rows)
            for f, source, target in (
                (0, vel.at[:, level, at, :], planes.at[0:2, to, s, :]),
                (2, thick.at[level, at, :], planes.at[2, to, s, :]),
                (3, trac.at[:, level, at, :], planes.at[3:5, to, s, :]),
                (5, mask.at[level, at, :], land.at[to, s, :]),
            ):
                groups[f].append(pltpu.make_async_copy(source, target, sem.at[f]))
    for f in groups:
        for copy in groups[f]:
            copy.start()
    total = rows * lat_count
    half = lax.broadcasted_iota(jnp.int32, (SUB, LANES), 0) % 2
    first = lax.axis_index("lat") * rows + half * half_rows
    for row in range(-2, half_rows + 2):
        ids = first + row
        folded = jnp.where(ids >= total, 2 * total - 1 - ids, ids)
        angle = jnp.pi * (folded.astype(F32) + 0.5) / total - jnp.pi / 2
        coriolis[row + PAD] = (CORIOLIS / HYPERVISCOSITY) * jnp.sin(angle)
    for f in range(6):
        for copy in groups.get(f, ()):
            copy.wait()
        if f == 5:
            break
        for row in range(PAD, half_rows + PAD) if f < ROLLED else ():
            value = planes[f, row]
            from_east[f, row] = pltpu.roll(value, width - 1, 1)
            from_west[f, row] = pltpu.roll(value, 1, 1)
    for row in range(PAD, half_rows + PAD):
        planes[5, row] = HYPERVISCOSITY * land[row].astype(F32)


def halo_columns(cols_a, cols_b, lon_even):
    def get(f):
        a, b = cols_a[f], cols_b[f]
        return halo_of(jnp.where(lon_even, a, b), jnp.where(lon_even, b, a))

    return get


def halo_of(from_east, from_west):
    lane = lax.broadcasted_iota(jnp.int32, (SUB, LANES), 1)

    def row(r):
        east = pltpu.roll(from_east, (LANES - HALO * r) % LANES, 1)
        west = pltpu.roll(from_west, LANES - HALO * (r + 1), 1)
        return jnp.where(lane < LANES // 2, east, west)

    return row


def rows_kernel(lat_count, planes, cols_a, cols_b, out_a, out_b):
    half_rows, width = planes.shape[1] - 2 * PAD, planes.shape[3]
    chunks = width // LANES
    lat = lax.axis_index("lat")
    lat_even = lat % 2 == 0
    lon_even = lax.axis_index("lon") % 2 == 0
    even = even_half(width + LANES)
    group = lax.broadcasted_iota(jnp.int32, (SUB, LANES), 1) // 8
    get = halo_columns(cols_a, cols_b, lon_even)
    column = [get(f) for f in range(6)]
    slots = [(f, m) for f in range(5) for m in range(2)] + [(5, None)]

    def whole(f, row):
        return jnp.concatenate([planes[f, row + PAD], column[f](row)], axis=1)

    def north(f, m):
        low = half_rows - HALO + 2 * m
        return jnp.where(even, pltpu.roll(whole(f, low + 1), SUB - 1, 0), whole(f, low))

    def south(f, m):
        return jnp.where(even, whole(f, 2 * m), pltpu.roll(whole(f, 2 * m + 1), 1, 0))

    def put(target, slot, value):
        for c in range(chunks):
            target[chunks * slot + c] = value[:, c * LANES : (c + 1) * LANES]

    def add_corner(corner, slot, value):
        return jnp.where(group == slot, pltpu.roll(value[:, width:], 8 * slot + HALO, 1), corner)

    corner_a = corner_b = jnp.zeros((SUB, LANES), F32)
    for slot, (f, m) in enumerate(slots):
        to_north = north(f, 1 if m is None else m)
        to_south = south(f, 0 if m is None else m)
        a = jnp.where(lat_even, to_north, to_south)
        b = jnp.where(lat_even, to_south, to_north)
        put(out_a, slot, a)
        put(out_b, slot, b)
        corner_a = add_corner(corner_a, slot, a)
        corner_b = add_corner(corner_b, slot, b)
    out_a[chunks * SLOTS] = corner_a
    out_b[chunks * SLOTS] = corner_b

    @pl.when(lat == lat_count - 1)
    def _():
        target = out_a if (lat_count - 1) % 2 == 0 else out_b
        corner = jnp.zeros((SUB, LANES), F32)
        for slot, (f, m) in enumerate(slots):
            value = north(f, 1 if m is None else 1 - m)
            value = -value if f < 2 else value
            mirrored = jnp.concatenate([flip_lanes(value[:, :width]), flip_lanes(value[:, width:])], axis=1)
            put(target, slot, mirrored)
            corner = add_corner(corner, slot, mirrored)
        target[chunks * SLOTS] = corner


def make_step(wide, sums, east_diff, press):
    scale = 1.0 / HYPERVISCOSITY
    keep_own = scale * (1.0 - 4.0 * DIFFUSION - 16.0 * HYPERVISCOSITY)
    keep_sum = scale * (DIFFUSION + 8.0 * HYPERVISCOSITY)
    advect = -0.5 * ADVECTION * scale
    slope = -0.5 * GRADIENT * scale
    converge = -0.5 * CONVERGENCE * scale
    level = lax.broadcasted_iota(jnp.int32, (SUB, wide), 0) // 2
    weight = slope / (level.astype(F32) + 1.0)
    below_one, below_two = level >= 1, level >= 2

    def shifts(value):
        return pltpu.roll(value, wide - 1, 1), pltpu.roll(value, 1, 1)

    def ahead(source, row, at, f, shifted, cut):
        to_east, to_west = shifted(f, row) if shifted else shifts(source(f, row))
        sums[f, at] = (to_east + to_west) + (source(f, row + 1) + source(f, row - 1))
        east_diff[f, at, :, :cut] = (to_east - to_west)[:, :cut]

    def weighed_down(thick, temp, salt):
        lanes = slice(0, thick.shape[-1])
        part = weight[:, lanes] * thick + ((0.08 * slope) * salt - (0.1 * slope) * temp)
        part = part + jnp.where(below_one[:, lanes], pltpu.roll(part, 2, 0), 0.0)
        return part + jnp.where(below_two[:, lanes], pltpu.roll(part, 4, 0), 0.0)

    def ahead_press(source, row, at, cut):
        press[at, :, :cut] = weighed_down(*(source(f, row)[:, :cut] for f in (2, 3, 4)))

    def update_row(source, ocean, turn, row, at, cut, emit, northward=None, roll_press=False, fields=range(5)):
        lanes = slice(0, cut)
        turn = jnp.concatenate([turn] * (cut // LANES), axis=1)
        u, v = source(0, row)[:, lanes], source(1, row)[:, lanes]
        along_u, along_v = advect * u, advect * v
        if northward is not None:
            along_v = along_v * northward[:, lanes]

        def add_on(f):
            if f == 0:
                if roll_press:
                    p_east, p_west = shifts(press[at])
                    return turn * v + (p_east - p_west)[:, lanes]
                slopes = [east_diff[field, at, :, lanes] for field in (2, 3, 4)]
                return turn * v + weighed_down(*slopes)
            if f == 1:
                rise = press[at + 1, :, lanes] - press[at - 1, :, lanes]
                if northward is not None:
                    rise = rise * northward[:, lanes]
                return rise - turn * u
            v_north = source(1, row + 1)[:, lanes] - source(1, row - 1)[:, lanes]
            if northward is not None:
                v_north = v_north * northward[:, lanes]
            return converge * (east_diff[0, at, :, lanes] + v_north)

        def one(f):
            here = sums[f, at]
            s_east, s_west = shifts(here)
            around = (s_east + s_west)[:, lanes] + (sums[f, at + 1, :, lanes] + sums[f, at - 1, :, lanes])
            dx = east_diff[f, at, :, lanes]
            dy = source(f, row + 1)[:, lanes] - source(f, row - 1)[:, lanes]
            value = keep_own * source(f, row)[:, lanes] + (keep_sum * here[:, lanes] - around)
            value = value + (along_u * dx + along_v * dy)
            if f < 3:
                value = value + add_on(f)
            emit(f, row, value * ocean)

        for f in fields:
            one(f)

    def ahead_row(source, row, at, cut, shifted=None):
        ahead_press(source, row, at, cut)
        for f in range(5):
            ahead(source, row, at, f, shifted, cut)

    return ahead_row, update_row


def swap_halves(value):
    even = even_half(value.shape[-1])
    return jnp.where(even, pltpu.roll(value, SUB - 1, 0), pltpu.roll(value, 1, 0))


def interior_kernel(
    planes,
    from_east,
    from_west,
    cols_a,
    cols_b,
    coriolis,
    after,
    out,
    middle,
    joint,
    ring,
    joint_sums,
    joint_diff,
    joint_press,
    outer,
    sides,
    second,
    centre,
    sums,
    east_diff,
    press,
):
    del after
    half_rows, width = planes.shape[1] - 2 * PAD, planes.shape[3]
    last = half_rows - 1
    wide = width + LANES
    lon_even = lax.axis_index("lon") % 2 == 0
    for f in range(6):
        a, b = cols_a[f], cols_b[f]
        sides[0, f] = jnp.where(lon_even, a, b)
        sides[1, f] = jnp.where(lon_even, b, a)

    def add_halo(row):
        for f in range(6):
            outer[f, row + PAD] = halo_of(sides[0, f], sides[1, f])(row)

    for row in range(4):
        add_halo(row)
    ahead_row, update_row = make_step(wide, sums, east_diff, press)
    even = even_half(wide)
    lane = lax.broadcasted_iota(jnp.int32, (SUB, LANES), 1)
    at_first, at_last = lane == 0, lane == LANES - 1

    def whole(f, row):
        return jnp.concatenate([planes[f, row + PAD], outer[f, row + PAD]], axis=1)

    def whole_shifted(f, row):
        at = row + PAD
        if f >= ROLLED:
            return pltpu.roll(whole(f, row), wide - 1, 1), pltpu.roll(whole(f, row), 1, 1)
        east, west, halo = from_east[f, at], from_west[f, at], outer[f, at]
        halo_east, halo_west = pltpu.roll(halo, LANES - 1, 1), pltpu.roll(halo, 1, 1)
        tail, head = east[:, width - LANES :], west[:, :LANES]
        east = [east[:, : width - LANES], jnp.where(at_last, halo_east, tail), jnp.where(at_last, tail, halo_east)]
        west = [jnp.where(at_first, halo_west, head), west[:, LANES:], jnp.where(at_first, head, halo_west)]
        return jnp.concatenate(east, axis=1), jnp.concatenate(west, axis=1)

    def keep(f, row, value):
        second[f, row + PAD] = value

    def halfway(f, row):
        return second[f, row + PAD]

    def write(f, row, value):
        out[f, row] = value

    def sweep(source, low, high, cut, emit, shifted=None):
        ahead_row(source, low - 1, low - 1 + PAD, cut, shifted)
        ahead_row(source, low, low + PAD, cut, shifted)

        def iteration(row, carry):
            if shifted:
                add_halo(row + 2)
            ahead_row(source, row + 1, row + 1 + PAD, cut, shifted)
            ocean, turn = whole(5, row)[:, :cut], coriolis[row + PAD]
            update_row(source, ocean, turn, row, row + PAD, cut, emit, roll_press=bool(shifted))
            return carry

        lax.fori_loop(low, high, iteration, 0, unroll=(high - low) // 2)

    def outer_pair(ref, i):
        return jnp.where(even, ref[i + PAD], ref[last - i + PAD])

    def inner_pair(ref, i):
        return jnp.where(even, ref[last - i + PAD], ref[i + PAD])

    def save_outer(step, i):
        for f in range(5):
            for k in range(2):
                joint_sums[step, f, k] = outer_pair(sums.at[f], i + k)
            joint_diff[step, f] = outer_pair(east_diff.at[f], i)
        for k in range(2):
            joint_press[step, k] = outer_pair(press, i + k)

    def take_inner(i):
        for f in range(5):
            sums[f, i + 1] = inner_pair(sums.at[f], i)
            east_diff[f, i + 1] = inner_pair(east_diff.at[f], i)
        press[i + 1] = inner_pair(press, i)

    def fold_inner():
        for f in range(5):
            sums[f, 0] = swap_halves(sums[f, 1])
        press[0] = swap_halves(press[1])

    sweep(whole, 2, half_rows - 2, wide, keep, whole_shifted)
    save_outer(0, 1)
    for i in range(4):
        for f in range(6):
            joint[f, i] = jnp.where(even, whole(f, i), whole(f, last - i))
        for f in range(5):
            ring[f, i] = outer_pair(second.at[f], 2 + i)

    def mirrored(f, i):
        if i < 0:
            return swap_halves(mirrored(f, -1 - i))
        return jnp.where(even, whole(f, last - i), whole(f, i))

    def mirrored_shifted(f, i):
        south, north = whole_shifted(f, last - i), whole_shifted(f, i)
        return [jnp.where(even, one, other) for one, other in zip(south, north)]

    north_odd = jnp.where(even, -1.0, 1.0)

    def turn_of(i):
        return jnp.where(even[:, :LANES], coriolis[last - i + PAD], coriolis[i + PAD])

    def keep_centre(f, i, value):
        centre[f, i + 2] = value
        centre[f, 1 - i] = swap_halves(value)

    ahead_row(mirrored, 0, 1, wide, mirrored_shifted)
    fold_inner()
    take_inner(1)
    take_inner(2)
    for i in range(2):
        update_row(mirrored, mirrored(5, i), turn_of(i), i, i + 1, wide, keep_centre, north_odd)

    sweep(halfway, HALO, half_rows - HALO, width, write)
    save_outer(1, 3)

    def centre_halfway(f, i):
        return centre[f, i + 2] if i < 2 else inner_pair(second.at[f], i)

    def keep_middle(f, i, value):
        middle[f, i] = value

    for i in range(3):
        ahead_row(centre_halfway, i, i + 1, width)
    fold_inner()
    take_inner(3)
    take_inner(4)
    for i in range(4):
        ocean = mirrored(5, i)[:, :width]
        update_row(centre_halfway, ocean, turn_of(i), i, i + 1, width, keep_middle, north_odd)


def edges_kernel(
    joint,
    ring,
    joint_sums,
    joint_diff,
    joint_press,
    middle,
    coriolis,
    done,
    rows_a,
    rows_b,
    vel_out,
    thick_out,
    trac_out,
    strip,
    first,
    second,
    sums,
    east_diff,
    press,
    sem,
):
    half_rows, width = done.shape[1], done.shape[3]
    wide = width + LANES
    chunks = width // LANES
    levels = SUB // 2

    def copies_out(source, source_row, row, count, groups=(0, 2, 3)):
        copies = []
        for level in range(levels):
            for half in range(2):
                s = 2 * level + half
                rows, to = pl.ds(source_row, count), pl.ds(half * half_rows + row, count)
                ends = {
                    0: (source.at[0:2, rows, s, :], vel_out.at[:, level, to, :]),
                    2: (source.at[2, rows, s, :], thick_out.at[level, to, :]),
                    3: (source.at[3:5, rows, s, :], trac_out.at[:, level, to, :]),
                }
                copies += [pltpu.make_async_copy(*ends[group], sem) for group in groups]
        for copy in copies:
            copy.start()
        return copies

    copies = copies_out(done, PAD, PAD, half_rows - 2 * PAD)
    for f in range(5):
        for i in range(HALO):
            strip[f, HALO + i] = done[f, HALO + i]
            strip[f, PAD + i] = done[f, half_rows - PAD + i]
    lat = lax.axis_index("lat")
    lat_even, southmost = lat % 2 == 0, lat == 0
    even, even_one = even_half(wide), even_half(LANES)
    even_out = even_half(width)
    corner_a, corner_b = rows_a[chunks * SLOTS], rows_b[chunks * SLOTS]

    def message(ref, corner, slot):
        parts = [ref[chunks * slot + c] for c in range(chunks)]
        return jnp.concatenate([*parts, pltpu.roll(corner, -(8 * slot + HALO) % LANES, 1)], axis=1)

    for f in range(6):
        reach = HALO if f < 5 else 2
        for m in range(reach // 2):
            slot, opposite = 2 * f + m, 2 * f + reach // 2 - 1 - m
            south = [message(ref, corner, slot) for ref, corner in ((rows_a, corner_a), (rows_b, corner_b))]
            north = [message(ref, corner, opposite) for ref, corner in ((rows_a, corner_a), (rows_b, corner_b))]
            from_south = jnp.where(southmost, 0.0, jnp.where(lat_even, south[1], south[0]))
            from_north = jnp.where(lat_even, north[0], north[1])
            row = 2 * m - reach
            first[f, row + HALO] = jnp.where(even, pltpu.roll(from_south, SUB - 1, 0), from_north)
            first[f, row + 1 + HALO] = jnp.where(even, from_south, pltpu.roll(from_north, 1, 0))

    def whole(f, i):
        return first[f, i + HALO] if i < 0 else joint[f, i]

    def halfway(f, i):
        return second[f, i + 2] if i < 2 else ring[f, i - 2]

    def keep(f, i, value):
        second[f, i + 2] = value

    def write(f, i, value):
        other = middle[f, i]
        strip[f, i] = jnp.where(even_out, value, other)
        strip[f, 2 * PAD - 1 - i] = jnp.where(even_out, other, value)

    ahead_row, update_row = make_step(wide, sums, east_diff, press)
    north_even = jnp.where(even, 1.0, -1.0)

    def sweep(source, step, low, cut, emit):
        high = low + 4
        for k in range(2):
            for f in range(5):
                sums[f, high - 1 + k + 4] = joint_sums[step, f, k]
            press[high - 1 + k + 4] = joint_press[step, k]
        for f in range(5):
            east_diff[f, high - 1 + 4] = joint_diff[step, f]
        for i in range(low - 1, low + 3):
            ahead_row(source, i, i + 4, cut)
        sent = []
        for fields in ((0, 1, 2, 3, 4),) if step == 0 else ((0, 1), (2,), (3, 4)):
            for i in range(low, high):
                turn = jnp.where(even_one, coriolis[i + PAD], coriolis[half_rows - 1 - i + PAD])
                ocean = whole(5, i)[:, :cut]
                update_row(source, ocean, turn, i, i + 4, cut, emit, north_even, fields=fields)
            if step == 1:
                sent += copies_out(strip, 0, 0, PAD, fields[:1])
                sent += copies_out(strip, PAD, half_rows - PAD, PAD, fields[:1])
        return sent

    sweep(whole, 0, -2, wide, keep)
    copies += sweep(halfway, 1, 0, width, write)
    for copy in copies:
        copy.wait()


def lat_pairs(parity, lat_count, lon_count):
    pairs = []
    for lat in range(lat_count):
        for lon in range(lon_count):
            to_lat, to_lon = (lat + 1 if lat % 2 == parity else lat - 1), lon
            if to_lat < 0:
                to_lat, to_lon = 0, lon ^ 1
            if to_lat == lat_count:
                to_lat, to_lon = lat, lon_count - 1 - lon
            pairs.append((lon * lat_count + lat, to_lon * lat_count + to_lat))
    return pairs


def lon_pairs(parity, lon_count):
    return [(i, (i + 1 if i % 2 == parity else i - 1) % lon_count) for i in range(lon_count)]


def shapes(*dims):
    return jax.ShapeDtypeStruct(dims, F32)


def body(lat_count, lon_count, velocity, thickness, tracers, land_mask):
    levels, rows, width = thickness.shape
    half_rows = rows // 2
    wide, tall = width + LANES, half_rows + 2 * PAD
    arguments = (velocity, thickness, tracers, land_mask)
    fields = [pltpu.with_memory_space_constraint(x, pltpu.HBM) for x in arguments]
    dma = pltpu.SemaphoreType.DMA

    def call(kernel, name, in_specs, outs, out_specs, scratch, flops):
        return pl.pallas_call(
            kernel,
            out_shape=outs,
            in_specs=in_specs,
            out_specs=out_specs,
            scratch_shapes=scratch,
            compiler_params=pltpu.CompilerParams(vmem_limit_bytes=24 * 2**20),
            cost_estimate=pl.CostEstimate(flops=flops, bytes_accessed=flops // 10, transcendentals=0),
            name=name,
        )

    columns = shapes(6, SUB, LANES)
    send_a, send_b = call(
        columns_kernel,
        "pack_columns",
        [HBM] * 4,
        (columns, columns),
        (VMEM, VMEM),
        [pltpu.VMEM((5, half_rows, SUB, 2 * LANES), F32), pltpu.VMEM((half_rows, SUB, 2 * LANES), jnp.int32), dma((6,))],
        10**6,
    )(*fields)
    cols_a = lax.ppermute(send_a, "lon", lon_pairs(0, lon_count))
    cols_b = lax.ppermute(send_b, "lon", lon_pairs(1, lon_count))

    block = shapes(ROLLED, tall, SUB, width)
    planes, from_east, from_west, coriolis = call(
        functools.partial(load_kernel, lat_count),
        "load_fields",
        [HBM, HBM, HBM, HBM, ANY],
        (shapes(6, tall, SUB, width), block, block, shapes(tall, SUB, LANES)),
        (VMEM,) * 4,
        [pltpu.VMEM((tall, SUB, width), jnp.int32), dma((6,))],
        10**8,
    )(*fields, send_a)

    message = shapes(SLOTS * (width // LANES) + 1, SUB, LANES)
    send_a, send_b = call(
        functools.partial(rows_kernel, lat_count),
        "pack_rows",
        [VMEM] * 3,
        (message, message),
        (VMEM, VMEM),
        [],
        10**6,
    )(planes, cols_a, cols_b)
    axes = ("lon", "lat")
    rows_a = lax.ppermute(send_a, axes, lat_pairs(0, lat_count, lon_count))
    rows_b = lax.ppermute(send_b, axes, lat_pairs(1, lat_count, lon_count))

    def work(length):
        tall_planes = pltpu.VMEM((5, length, SUB, wide), F32)
        return [tall_planes, tall_planes, pltpu.VMEM((length, SUB, wide), F32)]

    done, middle, *kept = call(
        interior_kernel,
        "interior",
        [VMEM] * 6 + [ANY],
        (
            shapes(5, half_rows, SUB, width),
            shapes(5, 4, SUB, width),
            shapes(6, 4, SUB, wide),
            shapes(5, 4, SUB, wide),
            shapes(2, 5, 2, SUB, wide),
            shapes(2, 5, SUB, wide),
            shapes(2, 2, SUB, wide),
        ),
        (VMEM,) * 7,
        [
            pltpu.VMEM((6, tall, SUB, LANES), F32),
            pltpu.VMEM((2, 6, SUB, LANES), F32),
            pltpu.VMEM((5, tall, SUB, wide), F32),
            pltpu.VMEM((5, 4, SUB, wide), F32),
            *work(tall),
        ],
        10**8,
    )(planes, from_east, from_west, cols_a, cols_b, coriolis, send_b)

    return call(
        edges_kernel,
        "edges",
        [VMEM] * 10,
        (shapes(*velocity.shape), shapes(*thickness.shape), shapes(*tracers.shape)),
        (HBM, HBM, HBM),
        [
            pltpu.VMEM((5, 2 * PAD, SUB, width), F32),
            pltpu.VMEM((6, HALO, SUB, wide), F32),
            pltpu.VMEM((5, 4, SUB, wide), F32),
            *work(10),
            dma,
        ],
        10**8,
    )(*kept, middle, coriolis, done, rows_a, rows_b)


def solution(mesh):
    specs = (P(None, None, "lat", "lon"), P(None, "lat", "lon"), P(None, None, "lat", "lon"))
    return jax.shard_map(
        functools.partial(body, mesh.shape["lat"], mesh.shape["lon"]),
        mesh=mesh,
        in_specs=(*specs, P(None, "lat", "lon")),
        out_specs=specs,
        check_vma=False,
    )
```

```python
import functools

import jax
import jax.numpy as jnp
from jax import lax
from jax.experimental import pallas as pl
from jax.experimental.pallas import tpu as pltpu
from jax.sharding import PartitionSpec as P

ADVECTION = 0.25
DIFFUSION = 0.05
HYPERVISCOSITY = 0.02
CORIOLIS = 0.3
GRADIENT = 0.2
CONVERGENCE = 0.3

HALO = 4
PAD = 8
LANES = 128
SUB = 8
SLOTS = 11
ROLLED = 3
F32 = jnp.float32
VMEM = pl.BlockSpec(memory_space=pltpu.VMEM)
HBM = pl.BlockSpec(memory_space=pltpu.HBM)
ANY = pl.BlockSpec(memory_space=pl.ANY)


def even_half(lanes):
    return lax.broadcasted_iota(jnp.int32, (SUB, lanes), 0) % 2 == 0


def flip_lanes(values):
    index = LANES - 1 - lax.broadcasted_iota(jnp.int32, (SUB, LANES), 1)
    chunks = range(0, values.shape[-1], LANES)
    parts = [jnp.take_along_axis(values[:, c : c + LANES], index, axis=1) for c in reversed(chunks)]
    return jnp.concatenate(parts, axis=1)


def columns_kernel(vel, thick, trac, mask, out_a, out_b, edges, land, sem):
    levels, rows, width = thick.shape
    half_rows = rows // 2
    groups = {0: [], 2: [], 3: [], 5: []}
    for side in range(2):
        lanes = pl.ds(side * (width - LANES), LANES)
        to = pl.ds(side * LANES, LANES)
        for level in range(levels):
            for half in range(2):
                at, s = pl.ds(half * half_rows, half_rows), 2 * level + half
                for f, source, target in (
                    (0, vel.at[:, level, at, lanes], edges.at[0:2, :, s, to]),
                    (2, thick.at[level, at, lanes], edges.at[2, :, s, to]),
                    (3, trac.at[:, level, at, lanes], edges.at[3:5, :, s, to]),
                    (5, mask.at[level, at, lanes], land.at[:, s, to]),
                ):
                    groups[f].append(pltpu.make_async_copy(source, target, sem.at[f]))
    for f in groups:
        for copy in groups[f]:
            copy.start()
    lon_even = lax.axis_index("lon") % 2 == 0
    group = lax.broadcasted_iota(jnp.int32, (SUB, LANES), 1) // HALO
    for f in range(6):
        for copy in groups.get(f, ()):
            copy.wait()
        west = east = jnp.zeros((SUB, LANES), F32)
        for row in range(half_rows):
            pair = edges[f, row] if f < 5 else HYPERVISCOSITY * land[row].astype(F32)
            here = group == row
            west = jnp.where(here, pltpu.roll(pair[:, :LANES], HALO * row % LANES, 1), west)
            east = jnp.where(here, pltpu.roll(pair[:, LANES:], HALO * (row + 1) % LANES, 1), east)
        out_a[f] = jnp.where(lon_even, east, west)
        out_b[f] = jnp.where(lon_even, west, east)


def load_kernel(lat_count, vel, thick, trac, mask, after, planes, from_east, from_west, coriolis, land, sem):
    del after
    levels, rows, width = thick.shape
    half_rows = rows // 2
    groups = {0: [], 2: [], 3: [], 5: []}
    for level in range(levels):
        for half in range(2):
            at, s = pl.ds(half * half_rows, half_rows), 2 * level + half
            to = pl.ds(PAD, half_rows)
            for f, source, target in (
                (0, vel.at[:, level, at, :], planes.at[0:2, to, s, :]),
                (2, thick.at[level, at, :], planes.at[2, to, s, :]),
                (3, trac.at[:, level, at, :], planes.at[3:5, to, s, :]),
                (5, mask.at[level, at, :], land.at[to, s, :]),
            ):
                groups[f].append(pltpu.make_async_copy(source, target, sem.at[f]))
    for f in groups:
        for copy in groups[f]:
            copy.start()
    total = rows * lat_count
    half = lax.broadcasted_iota(jnp.int32, (SUB, LANES), 0) % 2
    first = lax.axis_index("lat") * rows + half * half_rows
    for row in range(-2, half_rows + 2):
        ids = first + row
        folded = jnp.where(ids >= total, 2 * total - 1 - ids, ids)
        angle = jnp.pi * (folded.astype(F32) + 0.5) / total - jnp.pi / 2
        coriolis[row + PAD] = (CORIOLIS / HYPERVISCOSITY) * jnp.sin(angle)
    for f in range(6):
        for copy in groups.get(f, ()):
            copy.wait()
        if f == 5:
            break
        for row in range(PAD, half_rows + PAD) if f < ROLLED else ():
            value = planes[f, row]
            from_east[f, row] = pltpu.roll(value, width - 1, 1)
            from_west[f, row] = pltpu.roll(value, 1, 1)
    for row in range(PAD, half_rows + PAD):
        planes[5, row] = HYPERVISCOSITY * land[row].astype(F32)


def halo_columns(cols_a, cols_b, lon_even):
    def get(f):
        a, b = cols_a[f], cols_b[f]
        return halo_of(jnp.where(lon_even, a, b), jnp.where(lon_even, b, a))

    return get


def halo_of(from_east, from_west):
    lane = lax.broadcasted_iota(jnp.int32, (SUB, LANES), 1)

    def row(r):
        east = pltpu.roll(from_east, (LANES - HALO * r) % LANES, 1)
        west = pltpu.roll(from_west, LANES - HALO * (r + 1), 1)
        return jnp.where(lane < LANES // 2, east, west)

    return row


def rows_kernel(lat_count, planes, cols_a, cols_b, out_a, out_b):
    half_rows, width = planes.shape[1] - 2 * PAD, planes.shape[3]
    chunks = width // LANES
    lat = lax.axis_index("lat")
    lat_even = lat % 2 == 0
    lon_even = lax.axis_index("lon") % 2 == 0
    even = even_half(width + LANES)
    group = lax.broadcasted_iota(jnp.int32, (SUB, LANES), 1) // 8
    get = halo_columns(cols_a, cols_b, lon_even)
    column = [get(f) for f in range(6)]
    slots = [(f, m) for f in range(5) for m in range(2)] + [(5, None)]

    def whole(f, row):
        return jnp.concatenate([planes[f, row + PAD], column[f](row)], axis=1)

    def north(f, m):
        low = half_rows - HALO + 2 * m
        return jnp.where(even, pltpu.roll(whole(f, low + 1), SUB - 1, 0), whole(f, low))

    def south(f, m):
        return jnp.where(even, whole(f, 2 * m), pltpu.roll(whole(f, 2 * m + 1), 1, 0))

    def put(target, slot, value):
        for c in range(chunks):
            target[chunks * slot + c] = value[:, c * LANES : (c + 1) * LANES]

    def add_corner(corner, slot, value):
        return jnp.where(group == slot, pltpu.roll(value[:, width:], 8 * slot + HALO, 1), corner)

    corner_a = corner_b = jnp.zeros((SUB, LANES), F32)
    for slot, (f, m) in enumerate(slots):
        to_north = north(f, 1 if m is None else m)
        to_south = south(f, 0 if m is None else m)
        a = jnp.where(lat_even, to_north, to_south)
        b = jnp.where(lat_even, to_south, to_north)
        put(out_a, slot, a)
        put(out_b, slot, b)
        corner_a = add_corner(corner_a, slot, a)
        corner_b = add_corner(corner_b, slot, b)
    out_a[chunks * SLOTS] = corner_a
    out_b[chunks * SLOTS] = corner_b

    @pl.when(lat == lat_count - 1)
    def _():
        target = out_a if (lat_count - 1) % 2 == 0 else out_b
        corner = jnp.zeros((SUB, LANES), F32)
        for slot, (f, m) in enumerate(slots):
            value = north(f, 1 if m is None else 1 - m)
            value = -value if f < 2 else value
            mirrored = jnp.concatenate([flip_lanes(value[:, :width]), flip_lanes(value[:, width:])], axis=1)
            put(target, slot, mirrored)
            corner = add_corner(corner, slot, mirrored)
        target[chunks * SLOTS] = corner


def make_step(wide, sums, east_diff, press):
    scale = 1.0 / HYPERVISCOSITY
    keep_own = scale * (1.0 - 4.0 * DIFFUSION - 16.0 * HYPERVISCOSITY)
    keep_sum = scale * (DIFFUSION + 8.0 * HYPERVISCOSITY)
    advect = -0.5 * ADVECTION * scale
    slope = -0.5 * GRADIENT * scale
    converge = -0.5 * CONVERGENCE * scale
    level = lax.broadcasted_iota(jnp.int32, (SUB, wide), 0) // 2
    weight = slope / (level.astype(F32) + 1.0)
    below_one, below_two = level >= 1, level >= 2

    def shifts(value):
        return pltpu.roll(value, wide - 1, 1), pltpu.roll(value, 1, 1)

    def ahead(source, row, at, f, shifted, cut):
        to_east, to_west = shifted(f, row) if shifted else shifts(source(f, row))
        sums[f, at] = (to_east + to_west) + (source(f, row + 1) + source(f, row - 1))
        east_diff[f, at, :, :cut] = (to_east - to_west)[:, :cut]

    def weighed_down(thick, temp, salt):
        lanes = slice(0, thick.shape[-1])
        part = weight[:, lanes] * thick + ((0.08 * slope) * salt - (0.1 * slope) * temp)
        part = part + jnp.where(below_one[:, lanes], pltpu.roll(part, 2, 0), 0.0)
        return part + jnp.where(below_two[:, lanes], pltpu.roll(part, 4, 0), 0.0)

    def ahead_press(source, row, at, cut):
        press[at, :, :cut] = weighed_down(*(source(f, row)[:, :cut] for f in (2, 3, 4)))

    def update_row(source, ocean, turn, row, at, cut, emit, northward=None, roll_press=False, fields=range(5)):
        lanes = slice(0, cut)
        turn = jnp.concatenate([turn] * (cut // LANES), axis=1)
        u, v = source(0, row)[:, lanes], source(1, row)[:, lanes]
        along_u, along_v = advect * u, advect * v
        if northward is not None:
            along_v = along_v * northward[:, lanes]

        def add_on(f):
            if f == 0:
                if roll_press:
                    p_east, p_west = shifts(press[at])
                    return turn * v + (p_east - p_west)[:, lanes]
                slopes = [east_diff[field, at, :, lanes] for field in (2, 3, 4)]
                return turn * v + weighed_down(*slopes)
            if f == 1:
                rise = press[at + 1, :, lanes] - press[at - 1, :, lanes]
                if northward is not None:
                    rise = rise * northward[:, lanes]
                return rise - turn * u
            v_north = source(1, row + 1)[:, lanes] - source(1, row - 1)[:, lanes]
            if northward is not None:
                v_north = v_north * northward[:, lanes]
            return converge * (east_diff[0, at, :, lanes] + v_north)

        def one(f):
            here = sums[f, at]
            s_east, s_west = shifts(here)
            around = (s_east + s_west)[:, lanes] + (sums[f, at + 1, :, lanes] + sums[f, at - 1, :, lanes])
            dx = east_diff[f, at, :, lanes]
            dy = source(f, row + 1)[:, lanes] - source(f, row - 1)[:, lanes]
            value = keep_own * source(f, row)[:, lanes] + (keep_sum * here[:, lanes] - around)
            value = value + (along_u * dx + along_v * dy)
            if f < 3:
                value = value + add_on(f)
            emit(f, row, value * ocean)

        for f in fields:
            one(f)

    def ahead_row(source, row, at, cut, shifted=None):
        ahead_press(source, row, at, cut)
        for f in range(5):
            ahead(source, row, at, f, shifted, cut)

    return ahead_row, update_row


def swap_halves(value):
    even = even_half(value.shape[-1])
    return jnp.where(even, pltpu.roll(value, SUB - 1, 0), pltpu.roll(value, 1, 0))


def interior_kernel(
    planes,
    from_east,
    from_west,
    cols_a,
    cols_b,
    coriolis,
    after,
    out,
    middle,
    joint,
    ring,
    joint_sums,
    joint_diff,
    joint_press,
    outer,
    sides,
    second,
    centre,
    sums,
    east_diff,
    press,
):
    del after
    half_rows, width = planes.shape[1] - 2 * PAD, planes.shape[3]
    last = half_rows - 1
    wide = width + LANES
    lon_even = lax.axis_index("lon") % 2 == 0
    for f in range(6):
        a, b = cols_a[f], cols_b[f]
        sides[0, f] = jnp.where(lon_even, a, b)
        sides[1, f] = jnp.where(lon_even, b, a)

    def add_halo(row):
        for f in range(6):
            outer[f, row + PAD] = halo_of(sides[0, f], sides[1, f])(row)

    for row in range(4):
        add_halo(row)
    ahead_row, update_row = make_step(wide, sums, east_diff, press)
    even = even_half(wide)
    lane = lax.broadcasted_iota(jnp.int32, (SUB, LANES), 1)
    at_first, at_last = lane == 0, lane == LANES - 1

    def whole(f, row):
        return jnp.concatenate([planes[f, row + PAD], outer[f, row + PAD]], axis=1)

    def whole_shifted(f, row):
        at = row + PAD
        if f >= ROLLED:
            return pltpu.roll(whole(f, row), wide - 1, 1), pltpu.roll(whole(f, row), 1, 1)
        east, west, halo = from_east[f, at], from_west[f, at], outer[f, at]
        halo_east, halo_west = pltpu.roll(halo, LANES - 1, 1), pltpu.roll(halo, 1, 1)
        tail, head = east[:, width - LANES :], west[:, :LANES]
        east = [east[:, : width - LANES], jnp.where(at_last, halo_east, tail), jnp.where(at_last, tail, halo_east)]
        west = [jnp.where(at_first, halo_west, head), west[:, LANES:], jnp.where(at_first, head, halo_west)]
        return jnp.concatenate(east, axis=1), jnp.concatenate(west, axis=1)

    def keep(f, row, value):
        second[f, row + PAD] = value

    def halfway(f, row):
        return second[f, row + PAD]

    def write(f, row, value):
        out[f, row] = value

    def sweep(source, low, high, cut, emit, shifted=None):
        ahead_row(source, low - 1, low - 1 + PAD, cut, shifted)
        ahead_row(source, low, low + PAD, cut, shifted)

        def iteration(row, carry):
            if shifted:
                add_halo(row + 2)
            ahead_row(source, row + 1, row + 1 + PAD, cut, shifted)
            ocean, turn = whole(5, row)[:, :cut], coriolis[row + PAD]
            update_row(source, ocean, turn, row, row + PAD, cut, emit, roll_press=bool(shifted))
            return carry

        lax.fori_loop(low, high, iteration, 0, unroll=(high - low) // 2)

    def outer_pair(ref, i):
        return jnp.where(even, ref[i + PAD], ref[last - i + PAD])

    def inner_pair(ref, i):
        return jnp.where(even, ref[last - i + PAD], ref[i + PAD])

    def save_outer(step, i):
        for f in range(5):
            for k in range(2):
                joint_sums[step, f, k] = outer_pair(sums.at[f], i + k)
            joint_diff[step, f] = outer_pair(east_diff.at[f], i)
        for k in range(2):
            joint_press[step, k] = outer_pair(press, i + k)

    def take_inner(i):
        for f in range(5):
            sums[f, i + 1] = inner_pair(sums.at[f], i)
            east_diff[f, i + 1] = inner_pair(east_diff.at[f], i)
        press[i + 1] = inner_pair(press, i)

    def fold_inner():
        for f in range(5):
            sums[f, 0] = swap_halves(sums[f, 1])
        press[0] = swap_halves(press[1])

    sweep(whole, 2, half_rows - 2, wide, keep, whole_shifted)
    save_outer(0, 1)
    for i in range(4):
        for f in range(6):
            joint[f, i] = jnp.where(even, whole(f, i), whole(f, last - i))
        for f in range(5):
            ring[f, i] = outer_pair(second.at[f], 2 + i)

    def mirrored(f, i):
        if i < 0:
            return swap_halves(mirrored(f, -1 - i))
        return jnp.where(even, whole(f, last - i), whole(f, i))

    def mirrored_shifted(f, i):
        south, north = whole_shifted(f, last - i), whole_shifted(f, i)
        return [jnp.where(even, one, other) for one, other in zip(south, north)]

    north_odd = jnp.where(even, -1.0, 1.0)

    def turn_of(i):
        return jnp.where(even[:, :LANES], coriolis[last - i + PAD], coriolis[i + PAD])

    def keep_centre(f, i, value):
        centre[f, i + 2] = value
        centre[f, 1 - i] = swap_halves(value)

    ahead_row(mirrored, 0, 1, wide, mirrored_shifted)
    fold_inner()
    take_inner(1)
    take_inner(2)
    for i in range(2):
        update_row(mirrored, mirrored(5, i), turn_of(i), i, i + 1, wide, keep_centre, north_odd)

    sweep(halfway, HALO, half_rows - HALO, width, write)
    save_outer(1, 3)

    def centre_halfway(f, i):
        return centre[f, i + 2] if i < 2 else inner_pair(second.at[f], i)

    def keep_middle(f, i, value):
        middle[f, i] = value

    for i in range(3):
        ahead_row(centre_halfway, i, i + 1, width)
    fold_inner()
    take_inner(3)
    take_inner(4)
    for i in range(4):
        ocean = mirrored(5, i)[:, :width]
        update_row(centre_halfway, ocean, turn_of(i), i, i + 1, width, keep_middle, north_odd)


def edges_kernel(
    joint,
    ring,
    joint_sums,
    joint_diff,
    joint_press,
    middle,
    coriolis,
    done,
    rows_a,
    rows_b,
    vel_out,
    thick_out,
    trac_out,
    strip,
    first,
    second,
    sums,
    east_diff,
    press,
    sem,
):
    half_rows, width = done.shape[1], done.shape[3]
    wide = width + LANES
    chunks = width // LANES
    levels = SUB // 2

    def copies_out(source, source_row, row, count, groups=(0, 2, 3)):
        copies = []
        for level in range(levels):
            for half in range(2):
                s = 2 * level + half
                rows, to = pl.ds(source_row, count), pl.ds(half * half_rows + row, count)
                ends = {
                    0: (source.at[0:2, rows, s, :], vel_out.at[:, level, to, :]),
                    2: (source.at[2, rows, s, :], thick_out.at[level, to, :]),
                    3: (source.at[3:5, rows, s, :], trac_out.at[:, level, to, :]),
                }
                copies += [pltpu.make_async_copy(*ends[group], sem) for group in groups]
        for copy in copies:
            copy.start()
        return copies

    copies = copies_out(done, PAD, PAD, half_rows - 2 * PAD)
    for f in range(5):
        for i in range(HALO):
            strip[f, HALO + i] = done[f, HALO + i]
            strip[f, PAD + i] = done[f, half_rows - PAD + i]
    lat = lax.axis_index("lat")
    lat_even, southmost = lat % 2 == 0, lat == 0
    even, even_one = even_half(wide), even_half(LANES)
    even_out = even_half(width)
    corner_a, corner_b = rows_a[chunks * SLOTS], rows_b[chunks * SLOTS]

    def message(ref, corner, slot):
        parts = [ref[chunks * slot + c] for c in range(chunks)]
        return jnp.concatenate([*parts, pltpu.roll(corner, -(8 * slot + HALO) % LANES, 1)], axis=1)

    for f in range(6):
        reach = HALO if f < 5 else 2
        for m in range(reach // 2):
            slot, opposite = 2 * f + m, 2 * f + reach // 2 - 1 - m
            south = [message(ref, corner, slot) for ref, corner in ((rows_a, corner_a), (rows_b, corner_b))]
            north = [message(ref, corner, opposite) for ref, corner in ((rows_a, corner_a), (rows_b, corner_b))]
            from_south = jnp.where(southmost, 0.0, jnp.where(lat_even, south[1], south[0]))
            from_north = jnp.where(lat_even, north[0], north[1])
            row = 2 * m - reach
            first[f, row + HALO] = jnp.where(even, pltpu.roll(from_south, SUB - 1, 0), from_north)
            first[f, row + 1 + HALO] = jnp.where(even, from_south, pltpu.roll(from_north, 1, 0))

    def whole(f, i):
        return first[f, i + HALO] if i < 0 else joint[f, i]

    def halfway(f, i):
        return second[f, i + 2] if i < 2 else ring[f, i - 2]

    def keep(f, i, value):
        second[f, i + 2] = value

    def write(f, i, value):
        other = middle[f, i]
        strip[f, i] = jnp.where(even_out, value, other)
        strip[f, 2 * PAD - 1 - i] = jnp.where(even_out, other, value)

    ahead_row, update_row = make_step(wide, sums, east_diff, press)
    north_even = jnp.where(even, 1.0, -1.0)

    def sweep(source, step, low, cut, emit):
        high = low + 4
        for k in range(2):
            for f in range(5):
                sums[f, high - 1 + k + 4] = joint_sums[step, f, k]
            press[high - 1 + k + 4] = joint_press[step, k]
        for f in range(5):
            east_diff[f, high - 1 + 4] = joint_diff[step, f]
        for i in range(low - 1, low + 3):
            ahead_row(source, i, i + 4, cut)
        sent = []
        for fields in ((0, 1, 2, 3, 4),) if step == 0 else ((0, 1), (2,), (3, 4)):
            for i in range(low, high):
                turn = jnp.where(even_one, coriolis[i + PAD], coriolis[half_rows - 1 - i + PAD])
                ocean = whole(5, i)[:, :cut]
                update_row(source, ocean, turn, i, i + 4, cut, emit, north_even, fields=fields)
            if step == 1:
                sent += copies_out(strip, 0, 0, PAD, fields[:1])
                sent += copies_out(strip, PAD, half_rows - PAD, PAD, fields[:1])
        return sent

    sweep(whole, 0, -2, wide, keep)
    copies += sweep(halfway, 1, 0, width, write)
    for copy in copies:
        copy.wait()


def lat_pairs(parity, lat_count, lon_count):
    pairs = []
    for lat in range(lat_count):
        for lon in range(lon_count):
            to_lat, to_lon = (lat + 1 if lat % 2 == parity else lat - 1), lon
            if to_lat < 0:
                to_lat, to_lon = 0, lon ^ 1
            if to_lat == lat_count:
                to_lat, to_lon = lat, lon_count - 1 - lon
            pairs.append((lon * lat_count + lat, to_lon * lat_count + to_lat))
    return pairs


def lon_pairs(parity, lon_count):
    return [(i, (i + 1 if i % 2 == parity else i - 1) % lon_count) for i in range(lon_count)]


def shapes(*dims):
    return jax.ShapeDtypeStruct(dims, F32)


def body(lat_count, lon_count, velocity, thickness, tracers, land_mask):
    levels, rows, width = thickness.shape
    half_rows = rows // 2
    wide, tall = width + LANES, half_rows + 2 * PAD
    arguments = (velocity, thickness, tracers, land_mask)
    fields = [pltpu.with_memory_space_constraint(x, pltpu.HBM) for x in arguments]
    dma = pltpu.SemaphoreType.DMA

    def call(kernel, name, in_specs, outs, out_specs, scratch, flops):
        return pl.pallas_call(
            kernel,
            out_shape=outs,
            in_specs=in_specs,
            out_specs=out_specs,
            scratch_shapes=scratch,
            compiler_params=pltpu.CompilerParams(vmem_limit_bytes=24 * 2**20),
            cost_estimate=pl.CostEstimate(flops=flops, bytes_accessed=flops // 10, transcendentals=0),
            name=name,
        )

    columns = shapes(6, SUB, LANES)
    send_a, send_b = call(
        columns_kernel,
        "pack_columns",
        [HBM] * 4,
        (columns, columns),
        (VMEM, VMEM),
        [pltpu.VMEM((5, half_rows, SUB, 2 * LANES), F32), pltpu.VMEM((half_rows, SUB, 2 * LANES), jnp.int32), dma((6,))],
        10**6,
    )(*fields)
    cols_a = lax.ppermute(send_a, "lon", lon_pairs(0, lon_count))
    cols_b = lax.ppermute(send_b, "lon", lon_pairs(1, lon_count))

    block = shapes(ROLLED, tall, SUB, width)
    planes, from_east, from_west, coriolis = call(
        functools.partial(load_kernel, lat_count),
        "load_fields",
        [HBM, HBM, HBM, HBM, ANY],
        (shapes(6, tall, SUB, width), block, block, shapes(tall, SUB, LANES)),
        (VMEM,) * 4,
        [pltpu.VMEM((tall, SUB, width), jnp.int32), dma((6,))],
        10**8,
    )(*fields, send_a)

    message = shapes(SLOTS * (width // LANES) + 1, SUB, LANES)
    send_a, send_b = call(
        functools.partial(rows_kernel, lat_count),
        "pack_rows",
        [VMEM] * 3,
        (message, message),
        (VMEM, VMEM),
        [],
        10**6,
    )(planes, cols_a, cols_b)
    axes = ("lon", "lat")
    rows_a = lax.ppermute(send_a, axes, lat_pairs(0, lat_count, lon_count))
    rows_b = lax.ppermute(send_b, axes, lat_pairs(1, lat_count, lon_count))

    def work(length):
        tall_planes = pltpu.VMEM((5, length, SUB, wide), F32)
        return [tall_planes, tall_planes, pltpu.VMEM((length, SUB, wide), F32)]

    done, middle, *kept = call(
        interior_kernel,
        "interior",
        [VMEM] * 6 + [ANY],
        (
            shapes(5, half_rows, SUB, width),
            shapes(5, 4, SUB, width),
            shapes(6, 4, SUB, wide),
            shapes(5, 4, SUB, wide),
            shapes(2, 5, 2, SUB, wide),
            shapes(2, 5, SUB, wide),
            shapes(2, 2, SUB, wide),
        ),
        (VMEM,) * 7,
        [
            pltpu.VMEM((6, tall, SUB, LANES), F32),
            pltpu.VMEM((2, 6, SUB, LANES), F32),
            pltpu.VMEM((5, tall, SUB, wide), F32),
            pltpu.VMEM((5, 4, SUB, wide), F32),
            *work(tall),
        ],
        10**8,
    )(planes, from_east, from_west, cols_a, cols_b, coriolis, send_b)

    return call(
        edges_kernel,
        "edges",
        [VMEM] * 10,
        (shapes(*velocity.shape), shapes(*thickness.shape), shapes(*tracers.shape)),
        (HBM, HBM, HBM),
        [
            pltpu.VMEM((5, 2 * PAD, SUB, width), F32),
            pltpu.VMEM((6, HALO, SUB, wide), F32),
            pltpu.VMEM((5, 4, SUB, wide), F32),
            *work(10),
            dma,
        ],
        10**8,
    )(*kept, middle, coriolis, done, rows_a, rows_b)


def solution(mesh):
    specs = (P(None, None, "lat", "lon"), P(None, "lat", "lon"), P(None, None, "lat", "lon"))
    return jax.shard_map(
        functools.partial(body, mesh.shape["lat"], mesh.shape["lon"]),
        mesh=mesh,
        in_specs=(*specs, P(None, "lat", "lon")),
        out_specs=specs,
        check_vma=False,
    )
```
